32 devices in a mesh: ka: 4 (over x, core), tr: 2 (over y), tc: 4 (over z).
Axes of the slice: x: 2, y: 2, z: 4, core: 2. Of those that a mesh axis runs over, the one named last changes fastest.
Arguments:
- green_less: float32 [2, 4, 1024, 1024], P(None, 'ka', 'tr', 'tc'), may hold values from -6 to 6
- green_great: float32 [2, 4, 1024, 1024], P(None, 'ka', 'tr', 'tc'), may hold values from -6 to 6
- screened: float32 [2, 4, 1024, 1024], P(None, 'ka', 'tr', 'tc'), may hold values from -6 to 6
Outputs:
- collision: float32 [2, 4, 1024, 1024], P(None, 'ka', 'tr', 'tc')
- green_next: float32 [2, 4, 1024, 1024], P(None, 'ka', 'tr', 'tc')
The draws below stay inside these ranges and needn't reach their ends.
All inputs are finite; a program needn't handle non-finite values.
Results may differ from the reference program's by a relative error of at most 0.00012.
Values sent between devices are 32-bit elements; how exact they have to be, the bound alone decides.
No kernel may reach another device: no remote copies, remote signals or barrier semaphores. Data moves between devices by JAX's collectives and lax.ppermute only.
A program may use at most 64 MiB of HBM per device.

```python
import math
import jax
import jax.numpy as jnp
from jax import lax

K = 4
NT = 1024


def block_levels(rng, extent, split, smallest, largest):
    factor_of, own = 1.0, jax.random.fold_in(rng, 6)
    for axis_at, shards_of in split:
        draws = jnp.exp(jax.random.uniform(jax.random.fold_in(own, axis_at), (shards_of,), jnp.float32, smallest / len(split), largest / len(split)))
        factor_of = factor_of * jnp.repeat(draws, extent[axis_at] // shards_of).reshape([-1 if axis == axis_at else 1 for axis in range(len(extent))])
    return factor_of


def normal_values(rng, extent, spread, reach, split=(), kind=jnp.bfloat16):
    result = jax.random.normal(rng, extent, jnp.float32) * spread
    if len(split) > 0:
        result = block_levels(rng, extent, split, -0.22, 0.18) * result
    return jnp.clip(result, min=-reach, max=reach).astype(kind)


def setup_inputs(seed: int = 0) -> dict:
    seeds = jax.random.split(jax.random.key(seed), 4)
    green_less = normal_values(seeds[0], (2, K, NT, NT), 1.0, 6.0, ((1, 4), (2, 2), (3, 4)), jnp.float32)
    green_great = normal_values(seeds[1], (2, K, NT, NT), 1.0, 6.0, ((1, 4), (2, 2), (3, 4)), jnp.float32)
    screened = normal_values(seeds[2], (2, K, NT, NT), 1.0, 6.0, ((1, 4), (2, 2), (3, 4)), jnp.float32)
    return {"green_less": green_less, "green_great": green_great, "screened": screened}


def angle_tables(points):
    indices = jnp.arange(points, dtype=jnp.int32)
    phases = (indices[:, None] * indices[None, :]) % points
    angles = phases.astype(jnp.float32) * (2.0 * math.pi / points)
    return jnp.cos(angles), jnp.sin(angles)


def along_momenta(matrix_in, source):
    return jnp.tensordot(matrix_in, source, axes=1, precision=lax.Precision.HIGHEST)


def to_real(source, cosine_table, sine_table):
    factor = source.shape[1] ** -0.5
    real_part = along_momenta(cosine_table, source[0]) - along_momenta(sine_table, source[1])
    imag_part = along_momenta(cosine_table, source[1]) + along_momenta(sine_table, source[0])
    return jnp.stack([real_part, imag_part]) * factor


def to_momentum(source, cosine_table, sine_table):
    factor = source.shape[1] ** -0.5
    real_part = along_momenta(cosine_table, source[0]) + along_momenta(sine_table, source[1])
    imag_part = along_momenta(cosine_table, source[1]) - along_momenta(sine_table, source[0])
    return jnp.stack([real_part, imag_part]) * factor


def self_energy(less_tiles, great_tiles, screen_tiles, cosine_table, sine_table):
    lesser = to_real(less_tiles, cosine_table, sine_table)
    greater = to_real(great_tiles, cosine_table, sine_table)
    screen_real = to_real(screen_tiles, cosine_table, sine_table)
    polar_real = lesser[0] * greater[1] - lesser[1] * greater[0]
    polar_imag = lesser[0] * greater[0] + lesser[1] * greater[1]
    inter_real = screen_real[0] + polar_real
    inter_imag = screen_real[1] + polar_imag
    sigma_re = -(lesser[0] * inter_imag + lesser[1] * inter_real)
    sigma_im = lesser[0] * inter_real - lesser[1] * inter_imag
    return to_momentum(jnp.stack([sigma_re, sigma_im]), cosine_table, sine_table)


def matrix_product(left, right):
    return jnp.dot(left, right, preferred_element_type=jnp.float32, precision=lax.Precision.HIGHEST)


def reference(green_less, green_great, screened):
    points = green_less.shape[1]
    length = green_less.shape[2]
    blocks = length // 128
    cosine_table, sine_table = angle_tables(points)

    def split_rows(source):
        return jnp.moveaxis(source.reshape(2, points, blocks, 128, length), 2, 0)

    def one_block(pieces):
        return self_energy(pieces[0], pieces[1], pieces[2], cosine_table, sine_table)

    sigma_blocks = lax.map(one_block, (split_rows(green_less), split_rows(green_great), split_rows(screened)))
    sigma_tiles = jnp.moveaxis(sigma_blocks, 0, 2).reshape(2, points, length, length)

    def one_momentum(pieces):
        left_side, right_side = pieces
        real_part = matrix_product(left_side[0], right_side[0]) - matrix_product(left_side[1], right_side[1])
        imag_part = matrix_product(left_side[0], right_side[1]) + matrix_product(left_side[1], right_side[0])
        return jnp.stack([real_part, imag_part])

    products = lax.map(one_momentum, (jnp.moveaxis(sigma_tiles, 1, 0), jnp.moveaxis(green_less, 1, 0)))
    collision = jnp.moveaxis(products, 0, 1) * (NT ** -0.5)
    return collision, green_less + collision
```

```python
import math

import jax
import jax.numpy as jnp
from jax import lax
from jax.sharding import PartitionSpec as P

CHUNKS = 4
SUBLANES = 8


def times_i(value, power):
    real, imag = value
    return [(real, imag), (-imag, real), (-real, -imag), (imag, -real)][power % 4]


def add(left, right):
    return (left[0] + right[0], left[1] + right[1])


def subtract(left, right):
    return (left[0] - right[0], left[1] - right[1])


def twiddle(value, index, points, sign):
    if 4 * index % points == 0:
        return times_i(value, sign * (4 * index // points))
    angle = sign * 2.0 * math.pi * index / points
    cosine, sine = math.cos(angle), math.sin(angle)
    real, imag = value
    return (real * cosine - imag * sine, imag * cosine + real * sine)


def transform(values, sign):
    points = len(values)
    if points == 1:
        return values
    if points % 2:
        return [
            sum_of([twiddle(value, at * out % points, points, sign) for at, value in enumerate(values)])
            for out in range(points)
        ]
    even, odd = transform(values[::2], sign), transform(values[1::2], sign)
    odd = [twiddle(value, at, points, sign) for at, value in enumerate(odd)]
    return [add(e, o) for e, o in zip(even, odd)] + [subtract(e, o) for e, o in zip(even, odd)]


def sum_of(values):
    total = values[0]
    for value in values[1:]:
        total = add(total, value)
    return total


def self_energy(pieces, phases, scale):
    points = len(pieces)
    lesser = transform([(x[0, 0], x[0, 1]) for x in pieces], 1)
    greater = transform([(x[1, 0], x[1, 1]) for x in pieces], 1)
    screen = transform([(x[2, 0], x[2, 1]) for x in pieces], 1)
    sigma = []
    for r in range(points):
        less, great, inter = lesser[r], greater[r], screen[r]
        cosine, sine = phases[0][r], phases[1][r]
        polar_real = less[0] * great[1] - less[1] * great[0]
        polar_imag = less[0] * great[0] + less[1] * great[1]
        inter_real = inter[0] * cosine - inter[1] * sine + polar_real * points**-0.5
        inter_imag = inter[1] * cosine + inter[0] * sine + polar_imag * points**-0.5
        sigma.append(
            (
                -(less[0] * inter_imag + less[1] * inter_real) * scale,
                (less[0] * inter_real - less[1] * inter_imag) * scale,
            )
        )
    return [jnp.stack(value) for value in transform(sigma, -1)]


def shift(value, axis, moves):
    return lax.ppermute(value, axis, moves)


def body(green_less, green_great, screened):
    momenta, row_parts, col_parts = lax.axis_size("ka"), lax.axis_size("tr"), lax.axis_size("tc")
    own, row_at, col_at = lax.axis_index("ka"), lax.axis_index("tr"), lax.axis_index("tc")
    rows, cols = green_less.shape[2], green_less.shape[3]
    group = col_parts // row_parts
    half, member = col_at // group, col_at % group
    chunks = max(1, min(CHUNKS, rows // (momenta * SUBLANES)))
    step = rows // (momenta * chunks)
    length = rows * row_parts

    less = green_less[:, 0]
    blocks = less.reshape(2, group, cols, cols)
    sides = [lax.dynamic_index_in_dim(blocks, member, 1, False)]
    for gap in range(1, group):
        moves = [
            (part * group + m, part * group + (m + gap) % group) for part in range(row_parts) for m in range(group)
        ]
        sides.append(shift(lax.dynamic_index_in_dim(blocks, (member + gap) % group, 1, False), "tc", moves))
    panel = jnp.concatenate(sides, axis=2)
    panels = [panel] + [
        shift(panel, "tr", [(i, (i + gap) % row_parts) for i in range(row_parts)]) for gap in range(1, row_parts)
    ]
    stacked = jnp.stack(panels)
    right = jnp.concatenate(
        [
            lax.dynamic_index_in_dim(stacked, (row_at - half + gap) % row_parts, 0, False)
            for gap in range(row_parts)
        ],
        axis=1,
    )
    right = jnp.concatenate(
        [jnp.concatenate([right[0], right[1]], axis=1), jnp.concatenate([-right[1], right[0]], axis=1)], axis=0
    )

    angles = (own * jnp.arange(momenta) % momenta).astype(jnp.float32) * (2.0 * math.pi / momenta)
    phases = (jnp.cos(angles), jnp.sin(angles))
    scale = momenta**-1.5 * length**-0.5
    inputs = jnp.stack([less, green_great[:, 0], screened[:, 0]]).reshape(3, 2, chunks, momenta, step, cols)

    outs = []
    for chunk in range(chunks):
        source = inputs[:, :, chunk]
        pieces = [lax.dynamic_index_in_dim(source, own, 2, False)]
        for gap in range(1, momenta):
            piece = lax.dynamic_index_in_dim(source, (own - gap) % momenta, 2, False)
            pieces.append(shift(piece, "ka", [(s, (s - gap) % momenta) for s in range(momenta)]))
        sigma = self_energy(pieces, phases, scale)
        parts = [sigma[0]] + [
            shift(sigma[gap], "ka", [(s, (s + gap) % momenta) for s in range(momenta)]) for gap in range(1, momenta)
        ]
        mine = jnp.concatenate(parts, axis=1)
        sides = [mine] + [
            shift(mine, "tc", [(j, (j + group * gap) % col_parts) for j in range(col_parts)])
            for gap in range(1, row_parts)
        ]
        left = jnp.concatenate([side[at] for at in (0, 1) for side in sides], axis=1)
        product = jnp.dot(left, right, precision=lax.Precision.HIGH, preferred_element_type=jnp.float32)
        product = product.reshape(momenta * step, 2, group, cols)
        total = product[:, :, 0]
        for gap in range(1, group):
            moves = [
                (part * group + m, part * group + (m - gap) % group) for part in range(row_parts) for m in range(group)
            ]
            total = total + shift(product[:, :, gap], "tc", moves)
        outs.append(total.reshape(momenta, step, 2, cols))
    whole = jnp.stack(outs)
    order = (own - jnp.arange(momenta)) % momenta
    whole = jnp.take(whole, order, axis=1)
    collision = jnp.moveaxis(whole.reshape(rows, 2, cols), 1, 0)[:, None]
    return collision, green_less + collision


def solution(mesh):
    spec = P(None, "ka", "tr", "tc")
    return jax.shard_map(body, mesh=mesh, in_specs=(spec,) * 3, out_specs=(spec,) * 2, check_vma=False)
```

```python
import functools
import math

import jax
import jax.numpy as jnp
import numpy as np
from jax import lax
from jax.experimental import pallas as pl
from jax.experimental.pallas import tpu as pltpu
from jax.sharding import PartitionSpec as P

WEIGHTS = (2, 4, 4, 4, 2)
AHEAD = 2
SUBLANES, LANES = 8, 128
VMEM_LIMIT = 40 * 2**20
ANYWHERE = pl.BlockSpec(memory_space=pl.ANY)
IN_VMEM = pl.BlockSpec(memory_space=pltpu.VMEM)
IN_HBM = pl.BlockSpec(memory_space=pltpu.HBM)
IN_SMEM = pl.BlockSpec(memory_space=pltpu.SMEM)


def chunk_sizes(units):
    if units % sum(WEIGHTS):
        return [SUBLANES] * units
    return [SUBLANES * weight * units // sum(WEIGHTS) for weight in WEIGHTS]


def angle_tables(points):
    cosine = [[1.0, 0.0, -1.0, 0.0][4 * r // points] if 4 * r % points == 0 else math.cos(2 * math.pi * r / points) for r in range(points)]
    sine = [[0.0, 1.0, 0.0, -1.0][4 * r // points] if 4 * r % points == 0 else math.sin(2 * math.pi * r / points) for r in range(points)]
    return np.array([cosine, sine], np.float32)


def times_i(value, power):
    real, imag = value
    return [(real, imag), (-imag, real), (-real, -imag), (imag, -real)][power % 4]


def add(left, right):
    return (left[0] + right[0], left[1] + right[1])


def subtract(left, right):
    return (left[0] - right[0], left[1] - right[1])


def twiddle(value, index, points, sign):
    if 4 * index % points == 0:
        return times_i(value, sign * (4 * index // points))
    angle = sign * 2.0 * math.pi * index / points
    cosine, sine = math.cos(angle), math.sin(angle)
    real, imag = value
    return (real * cosine - imag * sine, imag * cosine + real * sine)


def transform(values, sign):
    points = len(values)
    if points == 1:
        return values
    if points % 2:
        return [
            functools.reduce(add, [twiddle(value, at * out % points, points, sign) for at, value in enumerate(values)])
            for out in range(points)
        ]
    even, odd = transform(values[::2], sign), transform(values[1::2], sign)
    odd = [twiddle(value, at, points, sign) for at, value in enumerate(odd)]
    return [add(e, o) for e, o in zip(even, odd)] + [subtract(e, o) for e, o in zip(even, odd)]


def at_rows(ref, start, size):
    return ref.at[:, 0, pl.ds(pl.multiple_of(start, SUBLANES), size), :]


def pack_copies(points, own, sources, pieces, sem, base, step):
    copies = []
    for gap in range(1, points):
        start = base + lax.rem(own - gap + points, points) * step
        for at, source in enumerate(sources):
            copies.append(pltpu.make_async_copy(at_rows(source, start, step), pieces[gap - 1].at[at], sem.at[len(copies)]))
    return copies


def pack_kernel(points, base, step, *refs):
    sources, pieces, sem = refs[:3], refs[3:-1], refs[-1]
    copies = pack_copies(points, lax.axis_index("ka"), sources, pieces, sem, base, step)
    for copy in copies:
        copy.start()
    for copy in copies:
        copy.wait()


def energy_kernel(points, base, step, later, scale, *refs):
    tables, sources, received = refs[0], refs[1:4], refs[4 : 3 + points]
    rest = refs[3 + points :]
    sigmas, pieces = rest[:points], rest[points:-3]
    mine, sem, own_sem = rest[-3:]
    own = lax.axis_index("ka")
    own_copies = [
        pltpu.make_async_copy(at_rows(source, base + own * step, step), mine.at[at], own_sem.at[at])
        for at, source in enumerate(sources)
    ]
    copies = pack_copies(points, own, sources, pieces, sem, *later) if later else []
    for copy in own_copies + copies:
        copy.start()
    for copy in own_copies:
        copy.wait()
    cosines = [tables[0, lax.rem(own * r, points)] for r in range(points)]
    sines = [tables[1, lax.rem(own * r, points)] for r in range(points)]
    blocks = [mine, *received]
    across = mine.shape[-1] // LANES
    root = points**-0.5

    def tile(index, carry):
        spot = (
            pl.ds(pl.multiple_of(lax.div(index, across) * SUBLANES, SUBLANES), SUBLANES),
            pl.ds(pl.multiple_of(lax.rem(index, across) * LANES, LANES), LANES),
        )
        lesser, greater, screen = (
            transform([(block[at, 0, *spot], block[at, 1, *spot]) for block in blocks], 1) for at in range(3)
        )
        values = []
        for r in range(points):
            less, great, inter = lesser[r], greater[r], screen[r]
            polar_real = less[0] * great[1] - less[1] * great[0]
            polar_imag = less[0] * great[0] + less[1] * great[1]
            inter_real = inter[0] * cosines[r] - inter[1] * sines[r] + polar_real * root
            inter_imag = inter[1] * cosines[r] + inter[0] * sines[r] + polar_imag * root
            values.append(
                (
                    (less[0] * inter_imag + less[1] * inter_real) * -scale,
                    (less[0] * inter_real - less[1] * inter_imag) * scale,
                )
            )
        for out, (real, imag) in zip(sigmas, transform(values, -1)):
            out[0, *spot] = real
            out[1, *spot] = imag
        return carry

    lax.fori_loop(0, step // SUBLANES * across, tile, 0)
    for copy in copies:
        copy.wait()


def assemble_kernel(points, step, *refs):
    parts, out = refs[:points], refs[points]
    own = lax.axis_index("ka")
    for gap in range(points):
        start = pl.multiple_of(lax.rem(own - gap + points, points) * step, SUBLANES)
        out[:, pl.ds(start, step), :] = parts[gap][...]


def split(value):
    high = value.astype(jnp.bfloat16)
    return high, (value - high.astype(jnp.float32)).astype(jnp.bfloat16)


def right_kernel(row_parts, group, *refs):
    pieces, high, low = refs[: row_parts * group], refs[-2], refs[-1]
    row_at, half = lax.axis_index("tr"), lax.axis_index("tc") // group
    depth, cols = pieces[0].shape[1:]
    for part in range(row_parts):
        place = lax.rem(half - row_at + part + row_parts, row_parts) * depth
        upper = pl.ds(pl.multiple_of(place, depth), depth)
        lower = pl.ds(pl.multiple_of(place + row_parts * depth, depth), depth)
        for gap in range(group):
            piece = pieces[part * group + gap]
            first = pl.ds(gap * cols, cols)
            second = pl.ds((group + gap) * cols, cols)
            real, imag = split(piece[0]), split(piece[1])
            for out, real_part, imag_part in zip((high, low), real, imag):
                out[upper, first] = real_part
                out[lower, second] = real_part
                out[upper, second] = imag_part
                out[lower, first] = -imag_part


def product_kernel(row_parts, group, *refs):
    sides, high, low, outs = refs[:row_parts], refs[row_parts], refs[row_parts + 1], refs[row_parts + 2 :]
    left = jnp.concatenate([side[at] for at in (0, 1) for side in sides], axis=1)
    left_high, left_low = split(left)
    cols = outs[0].shape[-1]
    for at in range(2):
        for gap in range(group):
            spot = pl.ds((at * group + gap) * cols, cols)
            right_high, right_low = high[:, spot], low[:, spot]
            dot = functools.partial(jnp.dot, preferred_element_type=jnp.float32)
            outs[gap][at] = dot(left_high, right_high) + (dot(left_high, right_low) + dot(left_low, right_high))


def final_kernel(group, sizes, *refs):
    count = len(sizes) * group
    parts, less, collision, after = refs[:count], refs[count], refs[-2], refs[-1]
    start = 0
    for at, size in enumerate(sizes):
        rows = pl.ds(start, size)
        total = parts[at * group][...]
        for part in parts[at * group + 1 : (at + 1) * group]:
            total = total + part[...]
        collision[:, 0, rows, :] = total
        after[:, 0, rows, :] = less[:, 0, rows, :] + total
        start += size


def call(kernel, out_shapes, in_specs, out_specs, args, scratch=(), after=()):
    count, skipped = len(args), len(after)

    def ordered(*refs):
        kernel(*refs[:count], *refs[count + skipped :])

    return pl.pallas_call(
        ordered,
        out_shape=out_shapes,
        in_specs=in_specs + [ANYWHERE] * skipped,
        out_specs=out_specs,
        scratch_shapes=scratch,
        cost_estimate=pl.CostEstimate(flops=1, bytes_accessed=1, transcendentals=0),
        compiler_params=pltpu.CompilerParams(vmem_limit_bytes=VMEM_LIMIT),
    )(*args, *after)


def body(green_less, green_great, screened):
    momenta, row_parts, col_parts = lax.axis_size("ka"), lax.axis_size("tr"), lax.axis_size("tc")
    col_at = lax.axis_index("tc")
    rows, cols = green_less.shape[2], green_less.shape[3]
    group = col_parts // row_parts
    member = col_at % group
    sizes = chunk_sizes(rows // momenta // SUBLANES)
    bases = [momenta * sum(sizes[:at]) for at in range(len(sizes))]
    length = rows * row_parts
    f32 = functools.partial(jax.ShapeDtypeStruct, dtype=jnp.float32)
    bf16 = functools.partial(jax.ShapeDtypeStruct, dtype=jnp.bfloat16)
    inputs = (green_less, green_great, screened)
    copies = 3 * (momenta - 1)
    scale = momenta**-1.5 * length**-0.5
    tables = jnp.asarray(angle_tables(momenta))

    def shift(value, axis, gap):
        if axis == "group":
            moves = [
                (part * group + m, part * group + (m + gap) % group) for part in range(row_parts) for m in range(group)
            ]
            return lax.ppermute(value, "tc", moves)
        if axis == "half":
            return lax.ppermute(value, "tc", [(j, (j + group * gap) % col_parts) for j in range(col_parts)])
        count = lax.axis_size(axis)
        return lax.ppermute(value, axis, [(s, (s + gap) % count) for s in range(count)])

    def send_pieces(pieces):
        return [shift(piece, "ka", -gap) for gap, piece in enumerate(pieces, 1)]

    def pack(at, after):
        step = sizes[at]
        return call(
            functools.partial(pack_kernel, momenta, bases[at], step),
            [f32((3, 2, step, cols))] * (momenta - 1),
            [IN_HBM] * 3,
            [ANYWHERE] * (momenta - 1),
            inputs,
            [pltpu.SemaphoreType.DMA((copies,))],
            after,
        )

    def energy(at, after):
        step, next_at = sizes[at], at + AHEAD
        later = (bases[next_at], sizes[next_at]) if next_at < len(sizes) else None
        outs = call(
            functools.partial(energy_kernel, momenta, bases[at], step, later, scale),
            [f32((2, step, cols))] * momenta + ([f32((3, 2, later[1], cols))] * (momenta - 1) if later else []),
            [IN_SMEM] + [IN_HBM] * 3 + [IN_VMEM] * (momenta - 1),
            [IN_VMEM] * momenta + ([ANYWHERE] * (momenta - 1) if later else []),
            (tables, *inputs, *received[at]),
            [
                pltpu.VMEM((3, 2, step, cols), jnp.float32),
                pltpu.SemaphoreType.DMA((copies,)),
                pltpu.SemaphoreType.DMA((3,)),
            ],
            after,
        )
        sigmas, pieces = outs[:momenta], outs[momenta:]
        parts = [sigmas[0]] + [shift(sigmas[gap], "ka", gap) for gap in range(1, momenta)]
        if later:
            received.append(send_pieces(pieces))
        return parts

    def assemble(at, parts, after):
        step = sizes[at]
        mine = call(
            functools.partial(assemble_kernel, momenta, step),
            f32((2, momenta * step, cols)),
            [IN_VMEM] * momenta,
            IN_VMEM,
            parts,
            (),
            after,
        )
        return [mine] + [shift(mine, "half", gap) for gap in range(1, row_parts)]

    def product(at, lefts, after):
        outs = call(
            functools.partial(product_kernel, row_parts, group),
            [f32((2, momenta * sizes[at], cols))] * group,
            [IN_VMEM] * (row_parts + 2),
            [IN_VMEM] * group,
            (*lefts, *right),
            (),
            after,
        )
        return [outs[0]] + [shift(outs[gap], "group", -gap) for gap in range(1, group)]

    received, last = [], ()
    for at in range(min(AHEAD, len(sizes))):
        pieces = pack(at, last)
        received.append(send_pieces(pieces))
        last = pieces[:1]

    blocks = green_less[:, 0].reshape(2, group, cols, cols)
    sides = [lax.dynamic_index_in_dim(blocks, member, 1, False)]
    for gap in range(1, group):
        sides.append(shift(lax.dynamic_index_in_dim(blocks, (member + gap) % group, 1, False), "group", gap))
    panels = list(sides)
    for gap in range(1, row_parts):
        panels += [shift(side, "tr", gap) for side in sides]
    extent = 2 * row_parts * cols

    lefts, results, right = [], [], None
    for at in range(len(sizes) + 1):
        if at < len(sizes):
            parts = energy(at, last)
            lefts.append(assemble(at, parts, ()))
            last = lefts[at][:1]
        if at == 1:
            right = call(
                functools.partial(right_kernel, row_parts, group),
                [bf16((extent, 2 * group * cols))] * 2,
                [IN_VMEM] * len(panels),
                [IN_VMEM] * 2,
                panels,
                (),
                last,
            )
        if at >= 1:
            results.append(product(at - 1, lefts[at - 1], last))
            last = results[-1][:1]

    return call(
        functools.partial(final_kernel, group, [momenta * step for step in sizes]),
        [f32(green_less.shape)] * 2,
        [IN_VMEM] * (len(sizes) * group + 1),
        [IN_VMEM] * 2,
        (*[part for result in results for part in result], green_less),
    )


def solution(mesh):
    spec = P(None, "ka", "tr", "tc")
    return jax.shard_map(body, mesh=mesh, in_specs=(spec,) * 3, out_specs=(spec,) * 2, check_vma=False)
```

```python
import functools
import math

import jax
import jax.numpy as jnp
import numpy as np
from jax import lax
from jax.experimental import pallas as pl
from jax.experimental.pallas import tpu as pltpu
from jax.sharding import PartitionSpec as P

WEIGHTS = (3, 5, 5, 3)
AHEAD = 2
SUBLANES, LANES = 8, 128
VMEM_LIMIT = 40 * 2**20
ANYWHERE = pl.BlockSpec(memory_space=pl.ANY)
IN_VMEM = pl.BlockSpec(memory_space=pltpu.VMEM)
IN_HBM = pl.BlockSpec(memory_space=pltpu.HBM)
IN_SMEM = pl.BlockSpec(memory_space=pltpu.SMEM)


def chunk_sizes(units):
    if units % sum(WEIGHTS):
        return [SUBLANES] * units
    return [SUBLANES * weight * units // sum(WEIGHTS) for weight in WEIGHTS]


def angle_tables(points):
    cosine = [[1.0, 0.0, -1.0, 0.0][4 * r // points] if 4 * r % points == 0 else math.cos(2 * math.pi * r / points) for r in range(points)]
    sine = [[0.0, 1.0, 0.0, -1.0][4 * r // points] if 4 * r % points == 0 else math.sin(2 * math.pi * r / points) for r in range(points)]
    return np.array([cosine, sine], np.float32)


def times_i(value, power):
    real, imag = value
    return [(real, imag), (-imag, real), (-real, -imag), (imag, -real)][power % 4]


def add(left, right):
    return (left[0] + right[0], left[1] + right[1])


def subtract(left, right):
    return (left[0] - right[0], left[1] - right[1])


def twiddle(value, index, points, sign):
    if 4 * index % points == 0:
        return times_i(value, sign * (4 * index // points))
    angle = sign * 2.0 * math.pi * index / points
    cosine, sine = math.cos(angle), math.sin(angle)
    real, imag = value
    return (real * cosine - imag * sine, imag * cosine + real * sine)


def transform(values, sign):
    points = len(values)
    if points == 1:
        return values
    if points % 2:
        return [
            functools.reduce(add, [twiddle(value, at * out % points, points, sign) for at, value in enumerate(values)])
            for out in range(points)
        ]
    even, odd = transform(values[::2], sign), transform(values[1::2], sign)
    odd = [twiddle(value, at, points, sign) for at, value in enumerate(odd)]
    return [add(e, o) for e, o in zip(even, odd)] + [subtract(e, o) for e, o in zip(even, odd)]


def at_rows(ref, start, size):
    return ref.at[:, 0, pl.ds(pl.multiple_of(start, SUBLANES), size), :]


def pack_copies(points, sources, pieces, sem, base, step):
    return [
        pltpu.make_async_copy(at_rows(source, base + part * step, step), pieces.at[part, at], sem.at[3 * part + at])
        for part in range(points)
        for at, source in enumerate(sources)
    ]


def pack_kernel(points, base, step, *refs):
    copies = pack_copies(points, refs[:3], *refs[3:], base, step)
    for copy in copies:
        copy.start()
    for copy in copies:
        copy.wait()


def energy_kernel(points, step, later, scale, *refs):
    tables, sources, received, sigmas, pieces = refs[0], refs[1:4], refs[4], refs[5 : 5 + points], refs[5 + points : -1]
    own = lax.axis_index("ka")
    copies = pack_copies(points, sources, pieces[0], refs[-1], *later) if later else []
    for copy in copies:
        copy.start()
    cosines = [tables[0, lax.rem(own * r, points)] for r in range(points)]
    sines = [tables[1, lax.rem(own * r, points)] for r in range(points)]
    blocks = [received.at[lax.rem(own + gap, points)] for gap in range(points)]
    across = received.shape[-1] // LANES
    root = points**-0.5

    def tile(index, carry):
        spot = (
            pl.ds(pl.multiple_of(lax.div(index, across) * SUBLANES, SUBLANES), SUBLANES),
            pl.ds(pl.multiple_of(lax.rem(index, across) * LANES, LANES), LANES),
        )
        lesser, greater, screen = (
            transform([(block[at, 0, *spot], block[at, 1, *spot]) for block in blocks], 1) for at in range(3)
        )
        values = []
        for r in range(points):
            less, great, inter = lesser[r], greater[r], screen[r]
            polar_real = less[0] * great[1] - less[1] * great[0]
            polar_imag = less[0] * great[0] + less[1] * great[1]
            inter_real = inter[0] * cosines[r] - inter[1] * sines[r] + polar_real * root
            inter_imag = inter[1] * cosines[r] + inter[0] * sines[r] + polar_imag * root
            values.append(
                (
                    (less[0] * inter_imag + less[1] * inter_real) * -scale,
                    (less[0] * inter_real - less[1] * inter_imag) * scale,
                )
            )
        for out, (real, imag) in zip(sigmas, transform(values, -1)):
            out[0, *spot] = real
            out[1, *spot] = imag
        return carry

    lax.fori_loop(0, step // SUBLANES * across, tile, 0)
    for copy in copies:
        copy.wait()


def assemble_kernel(points, step, *refs):
    parts, out = refs[:points], refs[points]
    own = lax.axis_index("ka")
    for gap in range(points):
        start = pl.multiple_of(lax.rem(own - gap + points, points) * step, SUBLANES)
        out[:, pl.ds(start, step), :] = parts[gap][...]


def split(value):
    high = value.astype(jnp.bfloat16)
    return high, (value - high.astype(jnp.float32)).astype(jnp.bfloat16)


def right_kernel(row_parts, group, *refs):
    pieces, high, low = refs[:group], refs[-2], refs[-1]
    half = lax.axis_index("tc") // group
    depth, cols = pieces[0].shape[2:]
    for part in range(row_parts):
        place = lax.rem(half - part + row_parts, row_parts) * depth
        upper = pl.ds(pl.multiple_of(place, depth), depth)
        lower = pl.ds(pl.multiple_of(place + row_parts * depth, depth), depth)
        for gap in range(group):
            piece = pieces[gap]
            first = pl.ds(gap * cols, cols)
            second = pl.ds((group + gap) * cols, cols)
            real, imag = split(piece[part, 0]), split(piece[part, 1])
            for out, real_part, imag_part in zip((high, low), real, imag):
                out[upper, first] = real_part
                out[lower, second] = real_part
                out[upper, second] = imag_part
                out[lower, first] = -imag_part


def product_kernel(row_parts, group, *refs):
    sides, high, low, outs = refs[:row_parts], refs[row_parts], refs[row_parts + 1], refs[row_parts + 2 :]
    left = jnp.concatenate([side[at] for at in (0, 1) for side in sides], axis=1)
    left_high, left_low = split(left)
    cols = outs[0].shape[-1]
    for at in range(2):
        for gap in range(group):
            spot = pl.ds((at * group + gap) * cols, cols)
            right_high, right_low = high[:, spot], low[:, spot]
            dot = functools.partial(jnp.dot, preferred_element_type=jnp.float32)
            outs[gap][at] = dot(left_high, right_high) + (dot(left_high, right_low) + dot(left_low, right_high))


def final_kernel(group, sizes, *refs):
    count = len(sizes) * group
    parts, less, collision, after = refs[:count], refs[count], refs[-2], refs[-1]
    start = 0
    for at, size in enumerate(sizes):
        rows = pl.ds(start, size)
        total = parts[at * group][...]
        for part in parts[at * group + 1 : (at + 1) * group]:
            total = total + part[...]
        collision[:, 0, rows, :] = total
        after[:, 0, rows, :] = less[:, 0, rows, :] + total
        start += size


def call(kernel, out_shapes, in_specs, out_specs, args, scratch=(), after=()):
    count, skipped = len(args), len(after)

    def ordered(*refs):
        kernel(*refs[:count], *refs[count + skipped :])

    return pl.pallas_call(
        ordered,
        out_shape=out_shapes,
        in_specs=in_specs + [ANYWHERE] * skipped,
        out_specs=out_specs,
        scratch_shapes=scratch,
        cost_estimate=pl.CostEstimate(flops=1, bytes_accessed=1, transcendentals=0),
        compiler_params=pltpu.CompilerParams(vmem_limit_bytes=VMEM_LIMIT),
    )(*args, *after)


def body(green_less, green_great, screened):
    momenta, row_parts, col_parts = lax.axis_size("ka"), lax.axis_size("tr"), lax.axis_size("tc")
    col_at = lax.axis_index("tc")
    rows, cols = green_less.shape[2], green_less.shape[3]
    group = col_parts // row_parts
    member = col_at % group
    sizes = chunk_sizes(rows // momenta // SUBLANES)
    bases = [momenta * sum(sizes[:at]) for at in range(len(sizes))]
    length = rows * row_parts
    f32 = functools.partial(jax.ShapeDtypeStruct, dtype=jnp.float32)
    bf16 = functools.partial(jax.ShapeDtypeStruct, dtype=jnp.bfloat16)
    inputs = (green_less, green_great, screened)
    copies = 3 * momenta
    scale = momenta**-1.5 * length**-0.5
    tables = jnp.asarray(angle_tables(momenta))

    def shift(value, axis, gap):
        if axis == "group":
            moves = [
                (part * group + m, part * group + (m + gap) % group) for part in range(row_parts) for m in range(group)
            ]
            return lax.ppermute(value, "tc", moves)
        if axis == "half":
            return lax.ppermute(value, "tc", [(j, (j + group * gap) % col_parts) for j in range(col_parts)])
        count = lax.axis_size(axis)
        return lax.ppermute(value, axis, [(s, (s + gap) % count) for s in range(count)])

    def send_pieces(pieces):
        return lax.all_to_all(pieces, "ka", split_axis=0, concat_axis=0, tiled=True)

    def pack(at, after):
        step = sizes[at]
        return call(
            functools.partial(pack_kernel, momenta, bases[at], step),
            f32((momenta, 3, 2, step, cols)),
            [IN_HBM] * 3,
            ANYWHERE,
            inputs,
            [pltpu.SemaphoreType.DMA((copies,))],
            after,
        )

    def energy(at, after):
        step, next_at = sizes[at], at + AHEAD
        later = (bases[next_at], sizes[next_at]) if next_at < len(sizes) else None
        outs = call(
            functools.partial(energy_kernel, momenta, step, later, scale),
            [f32((2, step, cols))] * momenta + ([f32((momenta, 3, 2, later[1], cols))] if later else []),
            [IN_SMEM] + [IN_HBM] * 3 + [IN_VMEM],
            [IN_VMEM] * momenta + ([ANYWHERE] if later else []),
            (tables, *inputs, received[at]),
            [pltpu.SemaphoreType.DMA((copies,))],
            after,
        )
        sigmas, pieces = outs[:momenta], outs[momenta:]
        parts = [sigmas[0]] + [shift(sigmas[gap], "ka", gap) for gap in range(1, momenta)]
        if later:
            received.append(send_pieces(pieces[0]))
        return parts

    def assemble(at, parts, after):
        step = sizes[at]
        mine = call(
            functools.partial(assemble_kernel, momenta, step),
            f32((2, momenta * step, cols)),
            [IN_VMEM] * momenta,
            IN_VMEM,
            parts,
            (),
            after,
        )
        return [mine] + [shift(mine, "half", gap) for gap in range(1, row_parts)]

    def product(at, lefts, after):
        outs = call(
            functools.partial(product_kernel, row_parts, group),
            [f32((2, momenta * sizes[at], cols))] * group,
            [IN_VMEM] * (row_parts + 2),
            [IN_VMEM] * group,
            (*lefts, *right),
            (),
            after,
        )
        return [outs[0]] + [shift(outs[gap], "group", -gap) for gap in range(1, group)]

    received, last = [], ()
    for at in range(min(AHEAD, len(sizes))):
        pieces = pack(at, last)
        received.append(send_pieces(pieces))
        last = (pieces,)

    blocks = green_less[:, 0].reshape(2, group, cols, cols)
    sides = [lax.dynamic_index_in_dim(blocks, member, 1, False)]
    for gap in range(1, group):
        sides.append(shift(lax.dynamic_index_in_dim(blocks, (member + gap) % group, 1, False), "group", gap))
    panels = [lax.all_gather(side, "tr") for side in sides]
    extent = 2 * row_parts * cols

    lefts, results, right = [], [], None
    for at in range(len(sizes) + 1):
        if at < len(sizes):
            parts = energy(at, last)
            lefts.append(assemble(at, parts, ()))
            last = lefts[at][:1]
        if at == 1:
            right = call(
                functools.partial(right_kernel, row_parts, group),
                [bf16((extent, 2 * group * cols))] * 2,
                [IN_VMEM] * len(panels),
                [IN_VMEM] * 2,
                panels,
                (),
                last,
            )
        if at >= 1:
            results.append(product(at - 1, lefts[at - 1], last))
            last = results[-1][:1]

    return call(
        functools.partial(final_kernel, group, [momenta * step for step in sizes]),
        [f32(green_less.shape)] * 2,
        [IN_VMEM] * (len(sizes) * group + 1),
        [IN_VMEM] * 2,
        (*[part for result in results for part in result], green_less),
    )


def solution(mesh):
    spec = P(None, "ka", "tr", "tc")
    return jax.shard_map(body, mesh=mesh, in_specs=(spec,) * 3, out_specs=(spec,) * 2, check_vma=False)
```

```python
import functools
import math

import jax
import jax.numpy as jnp
import numpy as np
from jax import lax
from jax.experimental import pallas as pl
from jax.experimental.pallas import tpu as pltpu
from jax.sharding import PartitionSpec as P

CORES = 2
WEIGHTS = (5, 10, 11, 6)
SUBLANES, LANES = 8, 128
VMEM_LIMIT = 40 * 2**20
ANYWHERE = pl.BlockSpec(memory_space=pl.ANY)
IN_VMEM = pl.BlockSpec(memory_space=pltpu.VMEM)
IN_HBM = pl.BlockSpec(memory_space=pltpu.HBM)
IN_SMEM = pl.BlockSpec(memory_space=pltpu.SMEM)


def chunk_sizes(units):
    if units % sum(WEIGHTS):
        return [SUBLANES * part for part in (units // 2, units - units // 2) if part]
    return [SUBLANES * weight * units // sum(WEIGHTS) for weight in WEIGHTS]


def angle_tables(points):
    cosine = [[1.0, 0.0, -1.0, 0.0][4 * r // points] if 4 * r % points == 0 else math.cos(2 * math.pi * r / points) for r in range(points)]
    sine = [[0.0, 1.0, 0.0, -1.0][4 * r // points] if 4 * r % points == 0 else math.sin(2 * math.pi * r / points) for r in range(points)]
    return np.array([cosine, sine], np.float32)


def times_i(value, power):
    real, imag = value
    return [(real, imag), (-imag, real), (-real, -imag), (imag, -real)][power % 4]


def add(left, right):
    return (left[0] + right[0], left[1] + right[1])


def subtract(left, right):
    return (left[0] - right[0], left[1] - right[1])


def twiddle(value, index, points, sign):
    if 4 * index % points == 0:
        return times_i(value, sign * (4 * index // points))
    angle = sign * 2.0 * math.pi * index / points
    cosine, sine = math.cos(angle), math.sin(angle)
    real, imag = value
    return (real * cosine - imag * sine, imag * cosine + real * sine)


def transform(values, sign):
    points = len(values)
    if points == 1:
        return values
    if points % 2:
        return [
            functools.reduce(add, [twiddle(value, at * out % points, points, sign) for at, value in enumerate(values)])
            for out in range(points)
        ]
    even, odd = transform(values[::2], sign), transform(values[1::2], sign)
    odd = [twiddle(value, at, points, sign) for at, value in enumerate(odd)]
    return [add(e, o) for e, o in zip(even, odd)] + [subtract(e, o) for e, o in zip(even, odd)]


def at_rows(ref, start, size):
    return ref.at[:, 0, pl.ds(pl.multiple_of(start, SUBLANES), size), :]


def pack_kernel(chips, base, step, *refs):
    sources, pieces, sem = refs[:3], refs[3:-1], refs[-1]
    chip = lax.axis_index("ka") // CORES
    copies = []
    for gap, piece in enumerate(pieces):
        start = base + lax.rem(chip - gap + chips, chips) * step
        for at, source in enumerate(sources):
            copies.append(pltpu.make_async_copy(at_rows(source, start, step), piece.at[at], sem.at[len(copies)]))
    for copy in copies:
        copy.start()
    for copy in copies:
        copy.wait()


def rotate(value, cosine, sine):
    return (value[0] * cosine - value[1] * sine, value[1] * cosine + value[0] * sine)


def energy_kernel(chips, scale, tables, *refs):
    here, other, sigmas = refs[:chips], refs[chips : 2 * chips], refs[2 * chips :]
    points = chips * CORES
    own = lax.axis_index("ka")
    side = (1 - 2 * lax.rem(own, CORES)).astype(jnp.float32)
    cosines = [tables[0, lax.rem(own * r, points)] for r in range(points)]
    sines = [tables[1, lax.rem(own * r, points)] for r in range(points)]
    step, across = here[0].shape[2], here[0].shape[3] // LANES
    root = points**-0.5

    def join(first, second):
        out = []
        for r in range(points):
            left, right = first[r % chips], second[r % chips]
            if 2 * r % points == 0:
                out.append(add(left, right) if r == 0 else subtract(left, right))
            elif 4 * r % points == 0:
                turned = (-right[1] * side, right[0] * side)
                out.append(add(left, turned) if 4 * r == points else subtract(left, turned))
            else:
                angle = 2.0 * math.pi * r / points
                out.append(add(left, rotate(right, math.cos(angle), math.sin(angle) * side)))
        return out

    def tile(index, carry):
        spot = (
            pl.ds(pl.multiple_of(lax.div(index, across) * SUBLANES, SUBLANES), SUBLANES),
            pl.ds(pl.multiple_of(lax.rem(index, across) * LANES, LANES), LANES),
        )
        lesser, greater, screen = (
            join(*(transform([(ref[at, 0, *spot], ref[at, 1, *spot]) for ref in group], 1) for group in (here, other)))
            for at in range(3)
        )
        values = []
        for r in range(points):
            less, great = lesser[r], greater[r]
            inter = screen[r] if r == 0 else rotate(screen[r], cosines[r], sines[r])
            polar_real = less[0] * great[1] - less[1] * great[0]
            polar_imag = less[0] * great[0] + less[1] * great[1]
            inter_real = inter[0] + polar_real * root
            inter_imag = inter[1] + polar_imag * root
            values.append(
                (
                    (less[0] * inter_imag + less[1] * inter_real) * -scale,
                    (less[0] * inter_real - less[1] * inter_imag) * scale,
                )
            )
        folded = [add(values[r], values[r + chips]) for r in range(chips)]
        for out, (real, imag) in zip(sigmas, transform(folded, -1)):
            out[0, *spot] = real
            out[1, *spot] = imag
        return carry

    lax.fori_loop(0, step // SUBLANES * across, tile, 0)


def split(value):
    high = value.astype(jnp.bfloat16)
    return high, (value - high.astype(jnp.float32)).astype(jnp.bfloat16)


def right_kernel(row_parts, group, *refs):
    pieces, high, low = refs[: row_parts * group], refs[-2], refs[-1]
    row_at, half = lax.axis_index("tr"), lax.axis_index("tc") // group
    depth, cols = pieces[0].shape[1:]
    for part in range(row_parts):
        place = lax.rem(half - row_at + part + row_parts, row_parts) * depth
        upper = pl.ds(pl.multiple_of(place, depth), depth)
        lower = pl.ds(pl.multiple_of(place + row_parts * depth, depth), depth)
        for gap in range(group):
            piece = pieces[part * group + gap]
            first = pl.ds(gap * cols, cols)
            second = pl.ds((group + gap) * cols, cols)
            real, imag = split(piece[0]), split(piece[1])
            for out, real_part, imag_part in zip((high, low), real, imag):
                out[upper, first] = real_part
                out[lower, second] = real_part
                out[upper, second] = imag_part
                out[lower, first] = -imag_part


def product_kernel(row_parts, group, chips, *refs):
    count = row_parts * chips
    sides, high, low, outs = refs[:count], refs[count], refs[count + 1], refs[count + 2 :]
    left = jnp.concatenate(
        [
            jnp.concatenate([sides[gap * row_parts + part][at] for at in (0, 1) for part in range(row_parts)], axis=1)
            for gap in range(chips)
        ],
        axis=0,
    )
    left_high, left_low = split(left)
    cols = outs[0].shape[-1]
    for at in range(2):
        for gap in range(group):
            spot = pl.ds((at * group + gap) * cols, cols)
            right_high, right_low = high[:, spot], low[:, spot]
            dot = functools.partial(jnp.dot, preferred_element_type=jnp.float32)
            outs[gap][at] = dot(left_high, right_high) + (dot(left_high, right_low) + dot(left_low, right_high))


def final_kernel(group, chips, sizes, *refs):
    count = len(sizes) * group
    parts, less, collision, after = refs[:count], refs[count], refs[-2], refs[-1]
    chip = lax.axis_index("ka") // CORES
    base = 0
    for at, step in enumerate(sizes):
        for gap in range(chips):
            start = base + lax.rem(chip - gap + chips, chips) * step
            rows = pl.ds(pl.multiple_of(start, SUBLANES), step)
            spot = pl.ds(gap * step, step)
            total = parts[at * group][:, spot, :]
            for part in parts[at * group + 1 : (at + 1) * group]:
                total = total + part[:, spot, :]
            collision[:, 0, rows, :] = total
            after[:, 0, rows, :] = less[:, 0, rows, :] + total
        base += chips * step


def call(kernel, out_shapes, in_specs, out_specs, args, scratch=(), after=()):
    count, skipped = len(args), len(after)

    def ordered(*refs):
        kernel(*refs[:count], *refs[count + skipped :])

    return pl.pallas_call(
        ordered,
        out_shape=out_shapes,
        in_specs=in_specs + [ANYWHERE] * skipped,
        out_specs=out_specs,
        scratch_shapes=scratch,
        cost_estimate=pl.CostEstimate(flops=1, bytes_accessed=1, transcendentals=0),
        compiler_params=pltpu.CompilerParams(vmem_limit_bytes=VMEM_LIMIT),
    )(*args, *after)


def body(green_less, green_great, screened):
    momenta, row_parts, col_parts = lax.axis_size("ka"), lax.axis_size("tr"), lax.axis_size("tc")
    member = lax.axis_index("tc") % (col_parts // row_parts)
    rows, cols = green_less.shape[2], green_less.shape[3]
    group, chips = col_parts // row_parts, momenta // CORES
    sizes = chunk_sizes(rows // chips // SUBLANES)
    bases = [chips * sum(sizes[:at]) for at in range(len(sizes))]
    f32 = functools.partial(jax.ShapeDtypeStruct, dtype=jnp.float32)
    bf16 = functools.partial(jax.ShapeDtypeStruct, dtype=jnp.bfloat16)
    inputs = (green_less, green_great, screened)
    scale = momenta**-1.5 * (rows * row_parts) ** -0.5
    tables = jnp.asarray(angle_tables(momenta))

    def to_chip(value, gap):
        moves = [
            (chip * CORES + core, (chip + gap) % chips * CORES + core) for chip in range(chips) for core in range(CORES)
        ]
        return lax.ppermute(value, "ka", moves)

    def to_core(value):
        return lax.ppermute(value, "ka", [(s, s + 1 - 2 * (s % CORES)) for s in range(momenta)])

    def to_panel(value, rows_on, cols_on):
        moves = []
        for i in range(row_parts):
            for j in range(col_parts):
                column = j // group * group + (j + cols_on) % group
                moves.append((i * col_parts + j, (i + rows_on) % row_parts * col_parts + column))
        return lax.ppermute(value, ("tr", "tc"), moves)

    def to_half(value, gap):
        return lax.ppermute(value, "tc", [(j, (j + group * gap) % col_parts) for j in range(col_parts)])

    def pack(at, after):
        step = sizes[at]
        return call(
            functools.partial(pack_kernel, chips, bases[at], step),
            [f32((3, 2, step, cols))] * chips,
            [IN_HBM] * 3,
            [ANYWHERE] * chips,
            inputs,
            [pltpu.SemaphoreType.DMA((3 * chips,))],
            after,
        )

    def forward(pieces):
        return [to_chip(pieces[gap], -gap) for gap in range(1, chips)], to_core(pieces[0])

    def energy(at, here, other, after):
        return call(
            functools.partial(energy_kernel, chips, scale),
            [f32((2, sizes[at], cols))] * chips,
            [IN_SMEM] + [IN_VMEM] * momenta,
            [IN_VMEM] * chips,
            (tables, *here, *other),
            (),
            after,
        )

    def product(at, lefts, after):
        outs = call(
            functools.partial(product_kernel, row_parts, group, chips),
            [f32((2, chips * sizes[at], cols))] * group,
            [IN_VMEM] * (len(lefts) + 2),
            [IN_VMEM] * group,
            (*lefts, *right),
            (),
            after,
        )
        return [outs[0]] + [to_panel(outs[gap], 0, -gap) for gap in range(1, group)]

    pieces = [pack(0, ())]
    sent = [forward(pieces[0])]

    blocks = green_less[:, 0].reshape(2, group, cols, cols)
    panels = []
    for rows_on in range(row_parts):
        for cols_on in range(group):
            block = lax.dynamic_index_in_dim(blocks, (member + cols_on) % group, 1, False)
            panels.append(to_panel(block, rows_on, cols_on) if rows_on + cols_on else block)
    extent = 2 * row_parts * cols

    lefts, results, right, last = [], [], None, ()
    for at in range(len(sizes) + 1):
        if at < len(sizes):
            across, beside = sent[at]
            if at + 1 < len(sizes):
                pieces.append(pack(at + 1, (across[0], *last)))
                sent.append(forward(pieces[at + 1]))
            here = [pieces[at][0], *across]
            other = [beside, *(to_core(piece) for piece in across)]
            sigmas = energy(at, here, other, last)
            owned = [sigmas[0]] + [to_chip(sigmas[gap], gap) for gap in range(1, chips)]
            lefts.append([part for own in owned for part in [own] + [to_half(own, gap) for gap in range(1, row_parts)]])
            last = sigmas[:1]
        if at == 1:
            right = call(
                functools.partial(right_kernel, row_parts, group),
                [bf16((extent, 2 * group * cols))] * 2,
                [IN_VMEM] * len(panels),
                [IN_VMEM] * 2,
                panels,
                (),
                last,
            )
        if at >= 1:
            results.append(product(at - 1, lefts[at - 1], last))
            last = results[-1][:1]

    return call(
        functools.partial(final_kernel, group, chips, sizes),
        [f32(green_less.shape)] * 2,
        [IN_VMEM] * (len(sizes) * group + 1),
        [IN_VMEM] * 2,
        (*[part for result in results for part in result], green_less),
    )


def solution(mesh):
    spec = P(None, "ka", "tr", "tc")
    return jax.shard_map(body, mesh=mesh, in_specs=(spec,) * 3, out_specs=(spec,) * 2, check_vma=False)
```

```python
import functools
import math

import jax
import jax.numpy as jnp
import numpy as np
from jax import lax
from jax.experimental import pallas as pl
from jax.experimental.pallas import tpu as pltpu
from jax.sharding import PartitionSpec as P

CORES = 2
WEIGHTS = (5, 10, 11, 6)
SUBLANES, LANES = 8, 128
VMEM_LIMIT = 40 * 2**20
FIRST_LIMIT = 62 * 2**20
ANYWHERE = pl.BlockSpec(memory_space=pl.ANY)
IN_VMEM = pl.BlockSpec(memory_space=pltpu.VMEM)
IN_HBM = pl.BlockSpec(memory_space=pltpu.HBM)
IN_SMEM = pl.BlockSpec(memory_space=pltpu.SMEM)


def chunk_sizes(units):
    if units % sum(WEIGHTS):
        return [SUBLANES * part for part in (units // 2, units - units // 2) if part]
    return [SUBLANES * weight * units // sum(WEIGHTS) for weight in WEIGHTS]


def angle_tables(points):
    cosine = [[1.0, 0.0, -1.0, 0.0][4 * r // points] if 4 * r % points == 0 else math.cos(2 * math.pi * r / points) for r in range(points)]
    sine = [[0.0, 1.0, 0.0, -1.0][4 * r // points] if 4 * r % points == 0 else math.sin(2 * math.pi * r / points) for r in range(points)]
    return np.array([cosine, sine], np.float32)


def times_i(value, power):
    real, imag = value
    return [(real, imag), (-imag, real), (-real, -imag), (imag, -real)][power % 4]


def add(left, right):
    return (left[0] + right[0], left[1] + right[1])


def subtract(left, right):
    return (left[0] - right[0], left[1] - right[1])


def twiddle(value, index, points, sign):
    if 4 * index % points == 0:
        return times_i(value, sign * (4 * index // points))
    angle = sign * 2.0 * math.pi * index / points
    cosine, sine = math.cos(angle), math.sin(angle)
    real, imag = value
    return (real * cosine - imag * sine, imag * cosine + real * sine)


def transform(values, sign):
    points = len(values)
    if points == 1:
        return values
    if points % 2:
        return [
            functools.reduce(add, [twiddle(value, at * out % points, points, sign) for at, value in enumerate(values)])
            for out in range(points)
        ]
    even, odd = transform(values[::2], sign), transform(values[1::2], sign)
    odd = [twiddle(value, at, points, sign) for at, value in enumerate(odd)]
    return [add(e, o) for e, o in zip(even, odd)] + [subtract(e, o) for e, o in zip(even, odd)]


def at_rows(ref, start, size):
    return ref.at[:, 0, pl.ds(pl.multiple_of(start, SUBLANES), size), :]


def pack_kernel(chips, base, step, passed, *refs):
    sources, pieces, sem = refs[:3], refs[3 + 2 * passed : -1], refs[-1]
    chip = lax.axis_index("ka") // CORES
    copies = []
    for gap, piece in enumerate(pieces):
        start = base + lax.rem(chip - gap + chips, chips) * step
        for at, source in enumerate(sources):
            copies.append(pltpu.make_async_copy(at_rows(source, start, step), piece.at[at], sem.at[len(copies)]))
    for copy in copies:
        copy.start()
    for copy in copies:
        copy.wait()


def rotate(value, cosine, sine):
    return (value[0] * cosine - value[1] * sine, value[1] * cosine + value[0] * sine)


def energy_kernel(chips, scale, tables, *refs):
    here, other, sigmas = refs[:chips], refs[chips : 2 * chips], refs[2 * chips :]
    points = chips * CORES
    own = lax.axis_index("ka")
    side = (1 - 2 * lax.rem(own, CORES)).astype(jnp.float32)
    cosines = [tables[0, lax.rem(own * r, points)] for r in range(points)]
    sines = [tables[1, lax.rem(own * r, points)] for r in range(points)]
    step, across = here[0].shape[2], here[0].shape[3] // LANES
    root = points**-0.5

    def join(first, second):
        out = []
        for r in range(points):
            left, right = first[r % chips], second[r % chips]
            if 2 * r % points == 0:
                out.append(add(left, right) if r == 0 else subtract(left, right))
            elif 4 * r % points == 0:
                turned = (-right[1] * side, right[0] * side)
                out.append(add(left, turned) if 4 * r == points else subtract(left, turned))
            else:
                angle = 2.0 * math.pi * r / points
                out.append(add(left, rotate(right, math.cos(angle), math.sin(angle) * side)))
        return out

    def tile(index, carry):
        spot = (
            pl.ds(pl.multiple_of(lax.div(index, across) * SUBLANES, SUBLANES), SUBLANES),
            pl.ds(pl.multiple_of(lax.rem(index, across) * LANES, LANES), LANES),
        )
        lesser, greater, screen = (
            join(*(transform([(ref[at, 0, *spot], ref[at, 1, *spot]) for ref in group], 1) for group in (here, other)))
            for at in range(3)
        )
        values = []
        for r in range(points):
            less, great = lesser[r], greater[r]
            inter = screen[r] if r == 0 else rotate(screen[r], cosines[r], sines[r])
            polar_real = less[0] * great[1] - less[1] * great[0]
            polar_imag = less[0] * great[0] + less[1] * great[1]
            inter_real = inter[0] + polar_real * root
            inter_imag = inter[1] + polar_imag * root
            values.append(
                (
                    (less[0] * inter_imag + less[1] * inter_real) * -scale,
                    (less[0] * inter_real - less[1] * inter_imag) * scale,
                )
            )
        folded = [add(values[r], values[r + chips]) for r in range(chips)]
        for out, (real, imag) in zip(sigmas, transform(folded, -1)):
            out[0, *spot] = real
            out[1, *spot] = imag
        return carry

    lax.fori_loop(0, step // SUBLANES * across, tile, 0)


def split(value):
    high = value.astype(jnp.bfloat16)
    return high, (value - high.astype(jnp.float32)).astype(jnp.bfloat16)


def right_kernel(row_parts, group, *refs):
    pieces, high, low = refs[: row_parts * group], refs[-2], refs[-1]
    row_at, half = lax.axis_index("tr"), lax.axis_index("tc") // group
    depth, cols = pieces[0].shape[1:]
    for part in range(row_parts):
        place = lax.rem(half - row_at + part + row_parts, row_parts) * depth
        upper = pl.ds(pl.multiple_of(place, depth), depth)
        lower = pl.ds(pl.multiple_of(place + row_parts * depth, depth), depth)
        for gap in range(group):
            piece = pieces[part * group + gap]
            first = pl.ds(gap * cols, cols)
            second = pl.ds((group + gap) * cols, cols)
            real, imag = split(piece[0]), split(piece[1])
            for out, real_part, imag_part in zip((high, low), real, imag):
                out[upper, first] = real_part
                out[lower, second] = real_part
                out[upper, second] = imag_part
                out[lower, first] = -imag_part


def product_kernel(row_parts, group, chips, *refs):
    count = row_parts * chips
    sides, high, low, outs = refs[:count], refs[count], refs[count + 1], refs[count + 2 :]
    left = jnp.concatenate(
        [
            jnp.concatenate([sides[gap * row_parts + part][at] for at in (0, 1) for part in range(row_parts)], axis=1)
            for gap in range(chips)
        ],
        axis=0,
    )
    left_high, left_low = split(left)
    cols = outs[0].shape[-1]
    for at in range(2):
        for gap in range(group):
            spot = pl.ds((at * group + gap) * cols, cols)
            right_high, right_low = high[:, spot], low[:, spot]
            dot = functools.partial(jnp.dot, preferred_element_type=jnp.float32)
            outs[gap][at] = dot(left_high, right_high) + (dot(left_high, right_low) + dot(left_low, right_high))


def final_kernel(group, chips, sizes, *refs):
    count = len(sizes) * group
    parts, less, collision, after = refs[:count], refs[count], refs[-2], refs[-1]
    chip = lax.axis_index("ka") // CORES
    base = 0
    for at, step in enumerate(sizes):
        for gap in range(chips):
            start = base + lax.rem(chip - gap + chips, chips) * step
            rows = pl.ds(pl.multiple_of(start, SUBLANES), step)
            spot = pl.ds(gap * step, step)
            total = parts[at * group][:, spot, :]
            for part in parts[at * group + 1 : (at + 1) * group]:
                total = total + part[:, spot, :]
            collision[:, 0, rows, :] = total
            after[:, 0, rows, :] = less[:, 0, rows, :] + total
        base += chips * step


def call(kernel, out_shapes, in_specs, out_specs, args, scratch=(), after=(), limit=VMEM_LIMIT, aliases=None):
    count, skipped = len(args), len(after)

    def ordered(*refs):
        kernel(*refs[:count], *refs[count + skipped :])

    return pl.pallas_call(
        ordered,
        out_shape=out_shapes,
        in_specs=in_specs + [ANYWHERE] * skipped,
        out_specs=out_specs,
        scratch_shapes=scratch,
        input_output_aliases=aliases or {},
        cost_estimate=pl.CostEstimate(flops=1, bytes_accessed=1, transcendentals=0),
        compiler_params=pltpu.CompilerParams(vmem_limit_bytes=limit),
    )(*args, *after)


def body(green_less, green_great, screened):
    momenta, row_parts, col_parts = lax.axis_size("ka"), lax.axis_size("tr"), lax.axis_size("tc")
    member = lax.axis_index("tc") % (col_parts // row_parts)
    rows, cols = green_less.shape[2], green_less.shape[3]
    group, chips = col_parts // row_parts, momenta // CORES
    sizes = chunk_sizes(rows // chips // SUBLANES)
    bases = [chips * sum(sizes[:at]) for at in range(len(sizes))]
    f32 = functools.partial(jax.ShapeDtypeStruct, dtype=jnp.float32)
    bf16 = functools.partial(jax.ShapeDtypeStruct, dtype=jnp.bfloat16)
    inputs = (green_less, green_great, screened)
    scale = momenta**-1.5 * (rows * row_parts) ** -0.5
    tables = jnp.asarray(angle_tables(momenta))

    def to_chip(value, gap):
        moves = [
            (chip * CORES + core, (chip + gap) % chips * CORES + core) for chip in range(chips) for core in range(CORES)
        ]
        return lax.ppermute(value, "ka", moves)

    def to_core(value):
        return lax.ppermute(value, "ka", [(s, s + 1 - 2 * (s % CORES)) for s in range(momenta)])

    def to_panel(value, rows_on, cols_on):
        moves = []
        for i in range(row_parts):
            for j in range(col_parts):
                column = j // group * group + (j + cols_on) % group
                moves.append((i * col_parts + j, (i + rows_on) % row_parts * col_parts + column))
        return lax.ppermute(value, ("tr", "tc"), moves)

    def to_half(value, gap):
        return lax.ppermute(value, "tc", [(j, (j + group * gap) % col_parts) for j in range(col_parts)])

    def pack(at, passed, after):
        step, count = sizes[at], len(passed)
        outs = call(
            functools.partial(pack_kernel, chips, bases[at], step, count),
            [f32(value.shape) for value in passed] + [f32((3, 2, step, cols))] * chips,
            [IN_HBM] * 3 + [ANYWHERE] * count,
            [ANYWHERE] * (count + chips),
            (*inputs, *passed),
            [pltpu.SemaphoreType.DMA((3 * chips,))],
            after,
            FIRST_LIMIT if at == 0 else VMEM_LIMIT,
            {3 + spot: spot for spot in range(count)},
        )
        return outs[count:], outs[:count]

    def gate(passed, after):
        count = len(passed)
        return call(
            lambda *refs: None,
            [f32(value.shape) for value in passed],
            [ANYWHERE] * count,
            [ANYWHERE] * count,
            passed,
            (),
            after,
            aliases={spot: spot for spot in range(count)},
        )

    def forward(pieces):
        return [to_chip(pieces[gap], -gap) for gap in range(1, chips)], to_core(pieces[0])

    def energy(at, here, other, after):
        return call(
            functools.partial(energy_kernel, chips, scale),
            [f32((2, sizes[at], cols))] * chips,
            [IN_SMEM] + [IN_VMEM] * momenta,
            [IN_VMEM] * chips,
            (tables, *here, *other),
            (),
            after,
        )

    def product(at, lefts, after):
        outs = call(
            functools.partial(product_kernel, row_parts, group, chips),
            [f32((2, chips * sizes[at], cols))] * group,
            [IN_VMEM] * (len(lefts) + 2),
            [IN_VMEM] * group,
            (*lefts, *right),
            (),
            after,
        )
        return [outs[0]] + [to_panel(outs[gap], 0, -gap) for gap in range(1, group)]

    pieces = [pack(0, (), ())[0]]
    sent = [forward(pieces[0])]

    blocks = green_less[:, 0].reshape(2, group, cols, cols)
    panels = []
    for rows_on in range(row_parts):
        for cols_on in range(group):
            block = lax.dynamic_index_in_dim(blocks, (member + cols_on) % group, 1, False)
            panels.append(to_panel(block, rows_on, cols_on) if rows_on + cols_on else block)
    extent = 2 * row_parts * cols

    lefts, results, last, arrived, returned = [], [], (), (), ()
    for at in range(len(sizes) + 1):
        if at < len(sizes):
            across, beside = sent[at]
            if at + 1 < len(sizes):
                fresh, across = pack(at + 1, across, (*arrived, *last))
                pieces.append(fresh)
                sent.append(forward(fresh))
            else:
                across = gate(across, (*arrived, *last))
            gates = panels[1:group]
            if at == 1:
                right = call(
                    functools.partial(right_kernel, row_parts, group),
                    [bf16((extent, 2 * group * cols))] * 2,
                    [IN_VMEM] * len(panels),
                    [IN_VMEM] * 2,
                    panels,
                    (),
                    across,
                )
                gates = right
            here = [pieces[at][0], *across]
            other = [beside, *(to_core(piece) for piece in across)]
            sigmas = energy(at, here, other, gates)
            owned = [sigmas[0]] + [to_chip(sigmas[gap], gap) for gap in range(1, chips)]
            lefts.append([part for own in owned for part in [own] + [to_half(own, gap) for gap in range(1, row_parts)]])
            returned = owned[1:2]
            arrived = (*returned, *lefts[at][1:2])
            if at == 0:
                arrived += tuple(panels[group:])
            last = sigmas[:1]
        if at >= 1:
            gates = (*last, *(returned if at + 1 == len(sizes) else ()), *(results[-1][1:] if results else ()))
            results.append(product(at - 1, lefts[at - 1], gates))
            last, returned = results[-1][:1], ()

    return call(
        functools.partial(final_kernel, group, chips, sizes),
        [f32(green_less.shape)] * 2,
        [IN_VMEM] * (len(sizes) * group + 1),
        [IN_VMEM] * 2,
        (*[part for result in results for part in result], green_less),
    )


def solution(mesh):
    spec = P(None, "ka", "tr", "tc")
    return jax.shard_map(body, mesh=mesh, in_specs=(spec,) * 3, out_specs=(spec,) * 2, check_vma=False)
```

```python
import functools
import math

import jax
import jax.numpy as jnp
import numpy as np
from jax import lax
from jax.experimental import pallas as pl
from jax.experimental.pallas import tpu as pltpu
from jax.sharding import PartitionSpec as P

CORES = 2
WEIGHTS = (5, 10, 11, 6)
SUBLANES, LANES = 8, 128
VMEM_LIMIT = 40 * 2**20
FIRST_LIMIT = 56 * 2**20
ANYWHERE = pl.BlockSpec(memory_space=pl.ANY)
IN_VMEM = pl.BlockSpec(memory_space=pltpu.VMEM)
IN_HBM = pl.BlockSpec(memory_space=pltpu.HBM)
IN_SMEM = pl.BlockSpec(memory_space=pltpu.SMEM)


def chunk_sizes(units):
    if units % sum(WEIGHTS):
        return [SUBLANES * part for part in (units // 2, units - units // 2) if part]
    return [SUBLANES * weight * units // sum(WEIGHTS) for weight in WEIGHTS]


def angle_tables(points):
    cosine = [[1.0, 0.0, -1.0, 0.0][4 * r // points] if 4 * r % points == 0 else math.cos(2 * math.pi * r / points) for r in range(points)]
    sine = [[0.0, 1.0, 0.0, -1.0][4 * r // points] if 4 * r % points == 0 else math.sin(2 * math.pi * r / points) for r in range(points)]
    return np.array([cosine, sine], np.float32)


def times_i(value, power):
    real, imag = value
    return [(real, imag), (-imag, real), (-real, -imag), (imag, -real)][power % 4]


def add(left, right):
    return (left[0] + right[0], left[1] + right[1])


def subtract(left, right):
    return (left[0] - right[0], left[1] - right[1])


def twiddle(value, index, points, sign):
    if 4 * index % points == 0:
        return times_i(value, sign * (4 * index // points))
    angle = sign * 2.0 * math.pi * index / points
    cosine, sine = math.cos(angle), math.sin(angle)
    real, imag = value
    return (real * cosine - imag * sine, imag * cosine + real * sine)


def transform(values, sign):
    points = len(values)
    if points == 1:
        return values
    if points % 2:
        return [
            functools.reduce(add, [twiddle(value, at * out % points, points, sign) for at, value in enumerate(values)])
            for out in range(points)
        ]
    even, odd = transform(values[::2], sign), transform(values[1::2], sign)
    odd = [twiddle(value, at, points, sign) for at, value in enumerate(odd)]
    return [add(e, o) for e, o in zip(even, odd)] + [subtract(e, o) for e, o in zip(even, odd)]


def at_rows(ref, start, size):
    return ref.at[:, 0, pl.ds(pl.multiple_of(start, SUBLANES), size), :]


def pack_kernel(chips, base, step, passed, *refs):
    sources, pieces, sem = refs[:3], refs[3 + 2 * passed : -1], refs[-1]
    chip = lax.axis_index("ka") // CORES
    copies = []
    for gap, piece in enumerate(pieces):
        start = base + lax.rem(chip - gap + chips, chips) * step
        for at, source in enumerate(sources):
            copies.append(pltpu.make_async_copy(at_rows(source, start, step), piece.at[at], sem.at[len(copies)]))
    for copy in copies:
        copy.start()
    for copy in copies:
        copy.wait()


def rotate(value, cosine, sine):
    return (value[0] * cosine - value[1] * sine, value[1] * cosine + value[0] * sine)


def energy_kernel(chips, scale, tables, *refs):
    here, other, returned, sigmas = refs[:chips], refs[chips : 2 * chips], refs[2 * chips : -chips], refs[-chips:]
    points = chips * CORES
    own = lax.axis_index("ka")
    side = (1 - 2 * lax.rem(own, CORES)).astype(jnp.float32)
    cosines = [tables[0, lax.rem(own * r, points)] for r in range(points)]
    sines = [tables[1, lax.rem(own * r, points)] for r in range(points)]
    step, across = here[0].shape[2], here[0].shape[3] // LANES
    root = points**-0.5

    def join(first, second):
        out = []
        for r in range(points):
            left, right = first[r % chips], second[r % chips]
            if 2 * r % points == 0:
                out.append(add(left, right) if r == 0 else subtract(left, right))
            elif 4 * r % points == 0:
                turned = (-right[1] * side, right[0] * side)
                out.append(add(left, turned) if 4 * r == points else subtract(left, turned))
            else:
                angle = 2.0 * math.pi * r / points
                out.append(add(left, rotate(right, math.cos(angle), math.sin(angle) * side)))
        return out

    def tile(index, carry):
        spot = (
            pl.ds(pl.multiple_of(lax.div(index, across) * SUBLANES, SUBLANES), SUBLANES),
            pl.ds(pl.multiple_of(lax.rem(index, across) * LANES, LANES), LANES),
        )
        lesser, greater, screen = (
            join(*(transform([(ref[at, 0, *spot], ref[at, 1, *spot]) for ref in group], 1) for group in (here, other)))
            for at in range(3)
        )
        values = []
        for r in range(points):
            less, great = lesser[r], greater[r]
            inter = screen[r] if r == 0 else rotate(screen[r], cosines[r], sines[r])
            polar_real = less[0] * great[1] - less[1] * great[0]
            polar_imag = less[0] * great[0] + less[1] * great[1]
            inter_real = inter[0] + polar_real * root
            inter_imag = inter[1] + polar_imag * root
            values.append(
                (
                    (less[0] * inter_imag + less[1] * inter_real) * -scale,
                    (less[0] * inter_real - less[1] * inter_imag) * scale,
                )
            )
        folded = [add(values[r], values[r + chips]) for r in range(chips)]
        for out, (real, imag) in zip(sigmas, transform(folded, -1)):
            out[0, *spot] = real
            out[1, *spot] = imag
        return carry

    lax.fori_loop(0, step // SUBLANES * across, tile, 0)
    place = step
    for value in returned:
        sigmas[0][:, place : place + value.shape[1], :] = value[...]
        place += value.shape[1]


def split(value):
    high = value.astype(jnp.bfloat16)
    return high, (value - high.astype(jnp.float32)).astype(jnp.bfloat16)


def right_kernel(group, *refs):
    pieces, high, low = refs[:group], refs[-2], refs[-1]
    half = lax.axis_index("tc") // group
    row_parts, _, depth, cols = pieces[0].shape
    for part in range(row_parts):
        place = lax.rem(half - part + row_parts, row_parts) * depth
        upper = pl.ds(pl.multiple_of(place, depth), depth)
        lower = pl.ds(pl.multiple_of(place + row_parts * depth, depth), depth)
        for gap, piece in enumerate(pieces):
            first = pl.ds(gap * cols, cols)
            second = pl.ds((group + gap) * cols, cols)
            real, imag = split(piece[part, 0]), split(piece[part, 1])
            for out, real_part, imag_part in zip((high, low), real, imag):
                out[upper, first] = real_part
                out[lower, second] = real_part
                out[upper, second] = imag_part
                out[lower, first] = -imag_part


def product_kernel(group, spans, *refs):
    count = len({part for parts, _, _ in spans for part in parts})
    high, low, outs = refs[count], refs[count + 1], refs[count + 2 :]
    left = jnp.concatenate(
        [
            jnp.concatenate([refs[part][at, start : start + size, :] for at in (0, 1) for part in parts], axis=1)
            for parts, start, size in spans
        ],
        axis=0,
    )
    left_high, left_low = split(left)
    cols = outs[0].shape[-1]
    for at in range(2):
        for gap in range(group):
            spot = pl.ds((at * group + gap) * cols, cols)
            right_high, right_low = high[:, spot], low[:, spot]
            dot = functools.partial(jnp.dot, preferred_element_type=jnp.float32)
            outs[gap][at] = dot(left_high, right_high) + (dot(left_high, right_low) + dot(left_low, right_high))


def final_kernel(group, chips, sizes, *refs):
    count = len(sizes) * group
    parts, less, collision, after = refs[:count], refs[count], refs[-2], refs[-1]
    chip = lax.axis_index("ka") // CORES
    base = 0
    for at, step in enumerate(sizes):
        for gap in range(chips):
            start = base + lax.rem(chip - gap + chips, chips) * step
            rows = pl.ds(pl.multiple_of(start, SUBLANES), step)
            spot = pl.ds(gap * step, step)
            total = parts[at * group][:, spot, :]
            for part in parts[at * group + 1 : (at + 1) * group]:
                total = total + part[:, spot, :]
            collision[:, 0, rows, :] = total
            after[:, 0, rows, :] = less[:, 0, rows, :] + total
        base += chips * step


def call(kernel, out_shapes, in_specs, out_specs, args, scratch=(), after=(), limit=VMEM_LIMIT, aliases=None):
    count, skipped = len(args), len(after)

    def ordered(*refs):
        kernel(*refs[:count], *refs[count + skipped :])

    return pl.pallas_call(
        ordered,
        out_shape=out_shapes,
        in_specs=in_specs + [ANYWHERE] * skipped,
        out_specs=out_specs,
        scratch_shapes=scratch,
        input_output_aliases=aliases or {},
        cost_estimate=pl.CostEstimate(flops=1, bytes_accessed=1, transcendentals=0),
        compiler_params=pltpu.CompilerParams(vmem_limit_bytes=limit),
    )(*args, *after)


def body(green_less, green_great, screened):
    momenta, row_parts, col_parts = lax.axis_size("ka"), lax.axis_size("tr"), lax.axis_size("tc")
    member = lax.axis_index("tc") % (col_parts // row_parts)
    rows, cols = green_less.shape[2], green_less.shape[3]
    group, chips = col_parts // row_parts, momenta // CORES
    sizes = chunk_sizes(rows // chips // SUBLANES)
    bases = [chips * sum(sizes[:at]) for at in range(len(sizes))]
    f32 = functools.partial(jax.ShapeDtypeStruct, dtype=jnp.float32)
    bf16 = functools.partial(jax.ShapeDtypeStruct, dtype=jnp.bfloat16)
    inputs = (green_less, green_great, screened)
    scale = momenta**-1.5 * (rows * row_parts) ** -0.5
    tables = jnp.asarray(angle_tables(momenta))

    def to_chip(value, gap):
        moves = [
            (chip * CORES + core, (chip + gap) % chips * CORES + core) for chip in range(chips) for core in range(CORES)
        ]
        return lax.ppermute(value, "ka", moves)

    def to_core(value):
        return lax.ppermute(value, "ka", [(s, s + 1 - 2 * (s % CORES)) for s in range(momenta)])

    def to_panel(value, rows_on, cols_on):
        moves = []
        for i in range(row_parts):
            for j in range(col_parts):
                column = j // group * group + (j + cols_on) % group
                moves.append((i * col_parts + j, (i + rows_on) % row_parts * col_parts + column))
        return lax.ppermute(value, ("tr", "tc"), moves)

    def to_half(value, gap):
        return lax.ppermute(value, "tc", [(j, (j + group * gap) % col_parts) for j in range(col_parts)])

    def pack(at, passed, after):
        step, count = sizes[at], len(passed)
        outs = call(
            functools.partial(pack_kernel, chips, bases[at], step, count),
            [f32(value.shape) for value in passed] + [f32((3, 2, step, cols))] * chips,
            [IN_HBM] * 3 + [ANYWHERE] * count,
            [ANYWHERE] * count + [ANYWHERE if at else IN_VMEM] * chips,
            (*inputs, *passed),
            [pltpu.SemaphoreType.DMA((3 * chips,))],
            after,
            FIRST_LIMIT if at == 0 else VMEM_LIMIT,
            {3 + spot: spot for spot in range(count)},
        )
        return outs[count:], outs[:count]

    def gate(passed, after):
        count = len(passed)
        return call(
            lambda *refs: None,
            [f32(value.shape) for value in passed],
            [ANYWHERE] * count,
            [ANYWHERE] * count,
            passed,
            (),
            after,
            aliases={spot: spot for spot in range(count)},
        )

    def forward(pieces):
        return [to_chip(pieces[gap], -gap) for gap in range(1, chips)], to_core(pieces[0])

    def energy(at, here, other, returned, after):
        step = sizes[at]
        height = step + sum(value.shape[1] for value in returned)
        return call(
            functools.partial(energy_kernel, chips, scale),
            [f32((2, height, cols))] + [f32((2, step, cols))] * (chips - 1),
            [IN_SMEM] + [IN_VMEM] * (momenta + len(returned)),
            [IN_VMEM] * chips,
            (tables, *here, *other, *returned),
            (),
            after,
        )

    def sides(value):
        return [value] + [to_half(value, gap) for gap in range(1, row_parts)]

    def product(at, after):
        step = sizes[at]
        arrays, spans = list(lefts[at]), [(range(row_parts), 0, step)]
        if at + 1 < len(sizes):
            arrays += lefts[at + 1]
            spans += [
                (range(row_parts, 2 * row_parts), sizes[at + 1] + gap * step, step) for gap in range(chips - 1)
            ]
        else:
            for gap in range(chips - 1):
                spans.append((range(len(arrays), len(arrays) + row_parts), 0, step))
                arrays += sides(returned[gap])
        outs = call(
            functools.partial(product_kernel, group, spans),
            [f32((2, chips * step, cols))] * group,
            [IN_VMEM] * (len(arrays) + 2),
            [IN_VMEM] * group,
            (*arrays, *right),
            (),
            after,
        )
        return [outs[0]] + [to_panel(outs[gap], 0, -gap) for gap in range(1, group)]

    pieces = [pack(0, (), ())[0]]
    sent = [forward(pieces[0])]

    blocks = green_less[:, 0].reshape(2, group, cols, cols)
    panels = []
    for gap in range(group):
        block = lax.dynamic_index_in_dim(blocks, (member + gap) % group, 1, False)
        panels.append(to_panel(block, 0, gap) if gap else block)
    early = panels[1:]
    panels = [lax.all_gather(panel, "tr") for panel in panels]
    extent = 2 * row_parts * cols

    lefts, results, returned, last = [], [], (), ()

    def add_product(after):
        at = len(results)
        results.append(product(at, (*after, *(results[at - 2][1:] if at >= 2 else ()))))
        return results[at][:1]

    for at, step in enumerate(sizes):
        across, beside = sent[at]
        if at + 1 < len(sizes):
            fresh, across = pack(at + 1, across, (*returned, *last, *(lefts[at - 1][1:] if at else ())))
            pieces.append(fresh)
            sent.append(forward(fresh))
        else:
            across = gate(across, (*returned, *last))
        here = [pieces[at][0], *across]
        other = [beside, *(to_core(piece) for piece in across)]
        sigmas = energy(at, here, other, returned, () if at else early)
        returned = [to_chip(sigmas[gap], gap) for gap in range(1, chips)]
        lefts.append(sides(sigmas[0]))
        last = sigmas[:1]
        if at == min(1, len(sizes) - 1):
            right = call(
                functools.partial(right_kernel, group),
                [bf16((extent, 2 * group * cols))] * 2,
                [IN_VMEM] * len(panels),
                [IN_VMEM] * 2,
                panels,
                (),
                last,
            )
        if at >= 2:
            last = add_product(last)
    while len(results) < len(sizes):
        last = add_product(last)

    return call(
        functools.partial(final_kernel, group, chips, sizes),
        [f32(green_less.shape)] * 2,
        [IN_VMEM] * (len(sizes) * group + 1),
        [IN_VMEM] * 2,
        (*[part for result in results for part in result], green_less),
    )


def solution(mesh):
    spec = P(None, "ka", "tr", "tc")
    return jax.shard_map(body, mesh=mesh, in_specs=(spec,) * 3, out_specs=(spec,) * 2, check_vma=False)
```

```python
import functools
import math

import jax
import jax.numpy as jnp
import numpy as np
from jax import lax
from jax.experimental import pallas as pl
from jax.experimental.pallas import tpu as pltpu
from jax.sharding import PartitionSpec as P

CORES = 2
WEIGHTS = (10, 10, 8, 4)
SUBLANES, LANES = 8, 128
VMEM_LIMIT = 40 * 2**20
FIRST_LIMIT = 56 * 2**20
ANYWHERE = pl.BlockSpec(memory_space=pl.ANY)
IN_VMEM = pl.BlockSpec(memory_space=pltpu.VMEM)
IN_HBM = pl.BlockSpec(memory_space=pltpu.HBM)
IN_SMEM = pl.BlockSpec(memory_space=pltpu.SMEM)


def chunk_sizes(units):
    if units % sum(WEIGHTS):
        return [SUBLANES * part for part in (units // 2, units - units // 2) if part]
    return [SUBLANES * weight * units // sum(WEIGHTS) for weight in WEIGHTS]


def angle_tables(points):
    cosine = [[1.0, 0.0, -1.0, 0.0][4 * r // points] if 4 * r % points == 0 else math.cos(2 * math.pi * r / points) for r in range(points)]
    sine = [[0.0, 1.0, 0.0, -1.0][4 * r // points] if 4 * r % points == 0 else math.sin(2 * math.pi * r / points) for r in range(points)]
    return np.array([cosine, sine], np.float32)


def times_i(value, power):
    real, imag = value
    return [(real, imag), (-imag, real), (-real, -imag), (imag, -real)][power % 4]


def add(left, right):
    return (left[0] + right[0], left[1] + right[1])


def subtract(left, right):
    return (left[0] - right[0], left[1] - right[1])


def twiddle(value, index, points, sign):
    if 4 * index % points == 0:
        return times_i(value, sign * (4 * index // points))
    angle = sign * 2.0 * math.pi * index / points
    cosine, sine = math.cos(angle), math.sin(angle)
    real, imag = value
    return (real * cosine - imag * sine, imag * cosine + real * sine)


def transform(values, sign):
    points = len(values)
    if points == 1:
        return values
    if points % 2:
        return [
            functools.reduce(add, [twiddle(value, at * out % points, points, sign) for at, value in enumerate(values)])
            for out in range(points)
        ]
    even, odd = transform(values[::2], sign), transform(values[1::2], sign)
    odd = [twiddle(value, at, points, sign) for at, value in enumerate(odd)]
    return [add(e, o) for e, o in zip(even, odd)] + [subtract(e, o) for e, o in zip(even, odd)]


def at_rows(ref, start, size):
    return ref.at[:, 0, pl.ds(pl.multiple_of(start, SUBLANES), size), :]


def pack_kernel(chips, base, step, passed, *refs):
    sources, pieces, sem = refs[:3], refs[3 + 2 * passed : -1], refs[-1]
    chip = lax.axis_index("ka") // CORES
    copies = []
    for gap, piece in enumerate(pieces):
        start = base + lax.rem(chip - gap + chips, chips) * step
        for at, source in enumerate(sources):
            copies.append(pltpu.make_async_copy(at_rows(source, start, step), piece.at[at], sem.at[len(copies)]))
    for copy in copies:
        copy.start()
    for copy in copies:
        copy.wait()


def rotate(value, cosine, sine):
    return (value[0] * cosine - value[1] * sine, value[1] * cosine + value[0] * sine)


def energy_kernel(chips, scale, tables, *refs):
    here, other, returned, sigmas = refs[:chips], refs[chips : 2 * chips], refs[2 * chips : -chips], refs[-chips:]
    points = chips * CORES
    own = lax.axis_index("ka")
    side = (1 - 2 * lax.rem(own, CORES)).astype(jnp.float32)
    cosines = [tables[0, lax.rem(own * r, points)] for r in range(points)]
    sines = [tables[1, lax.rem(own * r, points)] for r in range(points)]
    step, across = here[0].shape[2], here[0].shape[3] // LANES
    root = points**-0.5

    def join(first, second):
        out = []
        for r in range(points):
            left, right = first[r % chips], second[r % chips]
            if 2 * r % points == 0:
                out.append(add(left, right) if r == 0 else subtract(left, right))
            elif 4 * r % points == 0:
                turned = (-right[1] * side, right[0] * side)
                out.append(add(left, turned) if 4 * r == points else subtract(left, turned))
            else:
                angle = 2.0 * math.pi * r / points
                out.append(add(left, rotate(right, math.cos(angle), math.sin(angle) * side)))
        return out

    def tile(index, carry):
        spot = (
            pl.ds(pl.multiple_of(lax.div(index, across) * SUBLANES, SUBLANES), SUBLANES),
            pl.ds(pl.multiple_of(lax.rem(index, across) * LANES, LANES), LANES),
        )
        lesser, greater, screen = (
            join(*(transform([(ref[at, 0, *spot], ref[at, 1, *spot]) for ref in group], 1) for group in (here, other)))
            for at in range(3)
        )
        values = []
        for r in range(points):
            less, great = lesser[r], greater[r]
            inter = screen[r] if r == 0 else rotate(screen[r], cosines[r], sines[r])
            polar_real = less[0] * great[1] - less[1] * great[0]
            polar_imag = less[0] * great[0] + less[1] * great[1]
            inter_real = inter[0] + polar_real * root
            inter_imag = inter[1] + polar_imag * root
            values.append(
                (
                    (less[0] * inter_imag + less[1] * inter_real) * -scale,
                    (less[0] * inter_real - less[1] * inter_imag) * scale,
                )
            )
        folded = [add(values[r], values[r + chips]) for r in range(chips)]
        for out, (real, imag) in zip(sigmas, transform(folded, -1)):
            out[0, *spot] = real
            out[1, *spot] = imag
        return carry

    lax.fori_loop(0, step // SUBLANES * across, tile, 0)
    place = step
    for value in returned:
        sigmas[0][:, place : place + value.shape[1], :] = value[...]
        place += value.shape[1]


def split(value):
    high = value.astype(jnp.bfloat16)
    return high, (value - high.astype(jnp.float32)).astype(jnp.bfloat16)


def right_kernel(*refs):
    panels, outs = refs[:-2], refs[-2:]
    row_parts, (_, depth, width) = len(panels), panels[0].shape
    shift = lax.axis_index("tc") // (lax.axis_size("tc") // row_parts) - lax.axis_index("tr")
    first, second = pl.ds(0, width), pl.ds(width, width)
    for part, panel in enumerate(panels):
        place = lax.rem(shift + part + row_parts, row_parts) * depth
        upper = pl.ds(pl.multiple_of(place, depth), depth)
        lower = pl.ds(pl.multiple_of(place + row_parts * depth, depth), depth)
        for out, real, imag in zip(outs, split(panel[0]), split(panel[1])):
            out[upper, first] = real
            out[lower, second] = real
            out[upper, second] = imag
            out[lower, first] = -imag


def product_kernel(group, spans, *refs):
    count = len({part for parts, _, _ in spans for part in parts})
    high, low, outs = refs[count], refs[count + 1], refs[count + 2 :]
    left = jnp.concatenate(
        [
            jnp.concatenate([refs[part][at, start : start + size, :] for at in (0, 1) for part in parts], axis=1)
            for parts, start, size in spans
        ],
        axis=0,
    )
    left_high, left_low = split(left)
    cols = outs[0].shape[-1]
    for at in range(2):
        for gap in range(group):
            spot = pl.ds((at * group + gap) * cols, cols)
            right_high, right_low = high[:, spot], low[:, spot]
            dot = functools.partial(jnp.dot, preferred_element_type=jnp.float32)
            outs[gap][at] = dot(left_high, right_high) + (dot(left_high, right_low) + dot(left_low, right_high))


def final_kernel(group, chips, sizes, *refs):
    count = len(sizes) * group
    parts, less, collision, after = refs[:count], refs[count], refs[-2], refs[-1]
    chip = lax.axis_index("ka") // CORES
    base = 0
    for at, step in enumerate(sizes):
        for gap in range(chips):
            start = base + lax.rem(chip - gap + chips, chips) * step
            rows = pl.ds(pl.multiple_of(start, SUBLANES), step)
            spot = pl.ds(gap * step, step)
            total = parts[at * group][:, spot, :]
            for part in parts[at * group + 1 : (at + 1) * group]:
                total = total + part[:, spot, :]
            collision[:, 0, rows, :] = total
            after[:, 0, rows, :] = less[:, 0, rows, :] + total
        base += chips * step


def call(kernel, out_shapes, in_specs, out_specs, args, scratch=(), after=(), limit=VMEM_LIMIT, aliases=None):
    count, skipped = len(args), len(after)

    def ordered(*refs):
        kernel(*refs[:count], *refs[count + skipped :])

    return pl.pallas_call(
        ordered,
        out_shape=out_shapes,
        in_specs=in_specs + [ANYWHERE] * skipped,
        out_specs=out_specs,
        scratch_shapes=scratch,
        input_output_aliases=aliases or {},
        cost_estimate=pl.CostEstimate(flops=1, bytes_accessed=1, transcendentals=0),
        compiler_params=pltpu.CompilerParams(vmem_limit_bytes=limit),
    )(*args, *after)


def body(green_less, green_great, screened):
    momenta, row_parts, col_parts = lax.axis_size("ka"), lax.axis_size("tr"), lax.axis_size("tc")
    member = lax.axis_index("tc") % (col_parts // row_parts)
    rows, cols = green_less.shape[2], green_less.shape[3]
    group, chips = col_parts // row_parts, momenta // CORES
    sizes = chunk_sizes(rows // chips // SUBLANES)
    bases = [chips * sum(sizes[:at]) for at in range(len(sizes))]
    f32 = functools.partial(jax.ShapeDtypeStruct, dtype=jnp.float32)
    bf16 = functools.partial(jax.ShapeDtypeStruct, dtype=jnp.bfloat16)
    inputs = (green_less, green_great, screened)
    scale = momenta**-1.5 * (rows * row_parts) ** -0.5
    tables = jnp.asarray(angle_tables(momenta))

    def to_chip(value, gap):
        moves = [
            (chip * CORES + core, (chip + gap) % chips * CORES + core) for chip in range(chips) for core in range(CORES)
        ]
        return lax.ppermute(value, "ka", moves)

    def to_core(value):
        return lax.ppermute(value, "ka", [(s, s + 1 - 2 * (s % CORES)) for s in range(momenta)])

    def to_panel(value, rows_on, cols_on):
        moves = []
        for i in range(row_parts):
            for j in range(col_parts):
                column = j // group * group + (j + cols_on) % group
                moves.append((i * col_parts + j, (i + rows_on) % row_parts * col_parts + column))
        return lax.ppermute(value, ("tr", "tc"), moves)

    def to_half(value, gap):
        return lax.ppermute(value, "tc", [(j, (j + group * gap) % col_parts) for j in range(col_parts)])

    def pack(at, passed, after):
        step, count = sizes[at], len(passed)
        outs = call(
            functools.partial(pack_kernel, chips, bases[at], step, count),
            [f32(value.shape) for value in passed] + [f32((3, 2, step, cols))] * chips,
            [IN_HBM] * 3 + [ANYWHERE] * count,
            [ANYWHERE] * count + [ANYWHERE if at else IN_VMEM] * chips,
            (*inputs, *passed),
            [pltpu.SemaphoreType.DMA((3 * chips,))],
            after,
            FIRST_LIMIT if at == 0 else VMEM_LIMIT,
            {3 + spot: spot for spot in range(count)},
        )
        return outs[count:], outs[:count]

    def gate(passed, after):
        count = len(passed)
        return call(
            lambda *refs: None,
            [f32(value.shape) for value in passed],
            [ANYWHERE] * count,
            [ANYWHERE] * count,
            passed,
            (),
            after,
            aliases={spot: spot for spot in range(count)},
        )

    def forward(pieces):
        return [to_chip(pieces[gap], -gap) for gap in range(1, chips)], to_core(pieces[0])

    def energy(at, here, other, returned, after):
        step = sizes[at]
        height = step + sum(value.shape[1] for value in returned)
        return call(
            functools.partial(energy_kernel, chips, scale),
            [f32((2, height, cols))] + [f32((2, step, cols))] * (chips - 1),
            [IN_SMEM] + [IN_VMEM] * (momenta + len(returned)),
            [IN_VMEM] * chips,
            (tables, *here, *other, *returned),
            (),
            after,
        )

    def sides(value):
        return [value] + [to_half(value, gap) for gap in range(1, row_parts)]

    def product(at, after):
        step = sizes[at]
        arrays, spans = list(lefts[at]), [(range(row_parts), 0, step)]
        if at + 1 < len(sizes):
            arrays += lefts[at + 1]
            spans += [
                (range(row_parts, 2 * row_parts), sizes[at + 1] + gap * step, step) for gap in range(chips - 1)
            ]
        else:
            for gap in range(chips - 1):
                spans.append((range(len(arrays), len(arrays) + row_parts), 0, step))
                arrays += sides(returned[gap])
        outs = call(
            functools.partial(product_kernel, group, spans),
            [f32((2, chips * step, cols))] * group,
            [IN_VMEM] * (len(arrays) + 2),
            [IN_VMEM] * group,
            (*arrays, *right),
            (),
            after,
        )
        return [outs[0]] + [to_panel(outs[gap], 0, -gap) for gap in range(1, group)]

    pieces = [pack(0, (), ())[0]]
    sent = [forward(pieces[0])]

    blocks = green_less[:, 0].reshape(2, group, cols, cols)
    panels = []
    for gap in range(group):
        block = lax.dynamic_index_in_dim(blocks, (member + gap) % group, 1, False)
        panels.append(to_panel(block, 0, gap) if gap else block)
    early = panels[1:]
    panel = jnp.concatenate(panels, axis=2)
    panels = [panel] + [to_panel(panel, gap, 0) for gap in range(1, row_parts)]
    extent = 2 * row_parts * cols

    lefts, results, returned, last = [], [], (), ()

    def add_product(after):
        at = len(results)
        results.append(product(at, (*after, *(results[at - 2][1:] if at >= 2 else ()))))
        return results[at][:1]

    for at, step in enumerate(sizes):
        across, beside = sent[at]
        sent_over = (*lefts[at - 1][1:], *(early if at == 1 else ())) if at else ()
        if at + 1 < len(sizes):
            fresh, across = pack(at + 1, across, (*returned, *last, *sent_over))
            pieces.append(fresh)
            sent.append(forward(fresh))
        else:
            across = gate(across, (*returned, *last, *sent_over))
        here = [pieces[at][0], *across]
        other = [beside, *(to_core(piece) for piece in across)]
        ending = at >= 2 and at + 1 == len(sizes)
        if ending:
            last = add_product(across[:1])
        sigmas = energy(at, here, other, returned, last if ending else ())
        returned = [to_chip(sigmas[gap], gap) for gap in range(1, chips)]
        lefts.append(sides(sigmas[0]))
        last = sigmas[:1]
        if at == min(1, len(sizes) - 1):
            right = call(
                right_kernel,
                [bf16((extent, 2 * group * cols))] * 2,
                [IN_VMEM] * len(panels),
                [IN_VMEM] * 2,
                panels,
                (),
                last,
            )
        if at >= 2 and not ending:
            last = add_product(last)
    while len(results) < len(sizes):
        last = add_product(last)

    return call(
        functools.partial(final_kernel, group, chips, sizes),
        [f32(green_less.shape)] * 2,
        [IN_VMEM] * (len(sizes) * group + 1),
        [IN_VMEM] * 2,
        (*[part for result in results for part in result], green_less),
    )


def solution(mesh):
    spec = P(None, "ka", "tr", "tc")
    return jax.shard_map(body, mesh=mesh, in_specs=(spec,) * 3, out_specs=(spec,) * 2, check_vma=False)
```

```python
import functools
import math

import jax
import jax.numpy as jnp
import numpy as np
from jax import lax
from jax.experimental import pallas as pl
from jax.experimental.pallas import tpu as pltpu
from jax.sharding import PartitionSpec as P

CORES = 2
WEIGHTS = (5, 10, 11, 6)
SUBLANES, LANES = 8, 128
VMEM_LIMIT = 40 * 2**20
FIRST_LIMIT = 56 * 2**20
ANYWHERE = pl.BlockSpec(memory_space=pl.ANY)
IN_VMEM = pl.BlockSpec(memory_space=pltpu.VMEM)
IN_HBM = pl.BlockSpec(memory_space=pltpu.HBM)
IN_SMEM = pl.BlockSpec(memory_space=pltpu.SMEM)


def chunk_sizes(units):
    if units % sum(WEIGHTS):
        return [SUBLANES * part for part in (units // 2, units - units // 2) if part]
    return [SUBLANES * weight * units // sum(WEIGHTS) for weight in WEIGHTS]


def angle_tables(points):
    cosine = [[1.0, 0.0, -1.0, 0.0][4 * r // points] if 4 * r % points == 0 else math.cos(2 * math.pi * r / points) for r in range(points)]
    sine = [[0.0, 1.0, 0.0, -1.0][4 * r // points] if 4 * r % points == 0 else math.sin(2 * math.pi * r / points) for r in range(points)]
    return np.array([cosine, sine], np.float32)


def times_i(value, power):
    real, imag = value
    return [(real, imag), (-imag, real), (-real, -imag), (imag, -real)][power % 4]


def add(left, right):
    return (left[0] + right[0], left[1] + right[1])


def subtract(left, right):
    return (left[0] - right[0], left[1] - right[1])


def twiddle(value, index, points, sign):
    if 4 * index % points == 0:
        return times_i(value, sign * (4 * index // points))
    angle = sign * 2.0 * math.pi * index / points
    cosine, sine = math.cos(angle), math.sin(angle)
    real, imag = value
    return (real * cosine - imag * sine, imag * cosine + real * sine)


def transform(values, sign):
    points = len(values)
    if points == 1:
        return values
    if points % 2:
        return [
            functools.reduce(add, [twiddle(value, at * out % points, points, sign) for at, value in enumerate(values)])
            for out in range(points)
        ]
    even, odd = transform(values[::2], sign), transform(values[1::2], sign)
    odd = [twiddle(value, at, points, sign) for at, value in enumerate(odd)]
    return [add(e, o) for e, o in zip(even, odd)] + [subtract(e, o) for e, o in zip(even, odd)]


def at_rows(ref, start, size):
    return ref.at[:, 0, pl.ds(pl.multiple_of(start, SUBLANES), size), :]


def pack_kernel(chips, base, step, passed, *refs):
    sources, pieces, sem = refs[:3], refs[3 + 2 * passed : -1], refs[-1]
    chip = lax.axis_index("ka") // CORES
    copies = []
    for gap, piece in enumerate(pieces):
        start = base + lax.rem(chip - gap + chips, chips) * step
        for at, source in enumerate(sources):
            copies.append(pltpu.make_async_copy(at_rows(source, start, step), piece.at[at], sem.at[len(copies)]))
    for copy in copies:
        copy.start()
    for copy in copies:
        copy.wait()


def rotate(value, cosine, sine):
    return (value[0] * cosine - value[1] * sine, value[1] * cosine + value[0] * sine)


def energy_kernel(chips, scale, tables, *refs):
    here, other, sigmas = refs[:chips], refs[chips : 2 * chips], refs[2 * chips :]
    points = chips * CORES
    own = lax.axis_index("ka")
    side = (1 - 2 * lax.rem(own, CORES)).astype(jnp.float32)
    cosines = [tables[0, lax.rem(own * r, points)] for r in range(points)]
    sines = [tables[1, lax.rem(own * r, points)] for r in range(points)]
    step, across = here[0].shape[2], here[0].shape[3] // LANES
    root = points**-0.5

    def join(first, second):
        out = []
        for r in range(points):
            left, right = first[r % chips], second[r % chips]
            if 2 * r % points == 0:
                out.append(add(left, right) if r == 0 else subtract(left, right))
            elif 4 * r % points == 0:
                turned = (-right[1] * side, right[0] * side)
                out.append(add(left, turned) if 4 * r == points else subtract(left, turned))
            else:
                angle = 2.0 * math.pi * r / points
                out.append(add(left, rotate(right, math.cos(angle), math.sin(angle) * side)))
        return out

    def tile(index, carry):
        spot = (
            pl.ds(pl.multiple_of(lax.div(index, across) * SUBLANES, SUBLANES), SUBLANES),
            pl.ds(pl.multiple_of(lax.rem(index, across) * LANES, LANES), LANES),
        )
        lesser, greater, screen = (
            join(*(transform([(ref[at, 0, *spot], ref[at, 1, *spot]) for ref in group], 1) for group in (here, other)))
            for at in range(3)
        )
        values = []
        for r in range(points):
            less, great = lesser[r], greater[r]
            inter = screen[r] if r == 0 else rotate(screen[r], cosines[r], sines[r])
            polar_real = less[0] * great[1] - less[1] * great[0]
            polar_imag = less[0] * great[0] + less[1] * great[1]
            inter_real = inter[0] + polar_real * root
            inter_imag = inter[1] + polar_imag * root
            values.append(
                (
                    (less[0] * inter_imag + less[1] * inter_real) * -scale,
                    (less[0] * inter_real - less[1] * inter_imag) * scale,
                )
            )
        folded = [add(values[r], values[r + chips]) for r in range(chips)]
        for out, (real, imag) in zip(sigmas, transform(folded, -1)):
            out[0, *spot] = real
            out[1, *spot] = imag
        return carry

    lax.fori_loop(0, step // SUBLANES * across, tile, 0)


def split(value):
    high = value.astype(jnp.bfloat16)
    return high, (value - high.astype(jnp.float32)).astype(jnp.bfloat16)


def right_kernel(row_parts, group, *refs):
    pieces, high, low = refs[: row_parts * group], refs[-2], refs[-1]
    row_at, half = lax.axis_index("tr"), lax.axis_index("tc") // group
    depth, cols = pieces[0].shape[1:]
    for part in range(row_parts):
        place = lax.rem(half - row_at + part + row_parts, row_parts) * depth
        upper = pl.ds(pl.multiple_of(place, depth), depth)
        lower = pl.ds(pl.multiple_of(place + row_parts * depth, depth), depth)
        for gap in range(group):
            piece = pieces[part * group + gap]
            first = pl.ds(gap * cols, cols)
            second = pl.ds((group + gap) * cols, cols)
            real, imag = split(piece[0]), split(piece[1])
            for out, real_part, imag_part in zip((high, low), real, imag):
                out[upper, first] = real_part
                out[lower, second] = real_part
                out[upper, second] = imag_part
                out[lower, first] = -imag_part


def product_kernel(row_parts, group, chips, *refs):
    count = row_parts * chips
    sides, high, low, outs = refs[:count], refs[count], refs[count + 1], refs[count + 2 :]
    left = jnp.concatenate(
        [
            jnp.concatenate([sides[gap * row_parts + part][at] for at in (0, 1) for part in range(row_parts)], axis=1)
            for gap in range(chips)
        ],
        axis=0,
    )
    left_high, left_low = split(left)
    cols = outs[0].shape[-1]
    for at in range(2):
        for gap in range(group):
            spot = pl.ds((at * group + gap) * cols, cols)
            right_high, right_low = high[:, spot], low[:, spot]
            dot = functools.partial(jnp.dot, preferred_element_type=jnp.float32)
            outs[gap][at] = dot(left_high, right_high) + (dot(left_high, right_low) + dot(left_low, right_high))


def final_kernel(group, chips, sizes, *refs):
    count = len(sizes) * group
    parts, less, collision, after = refs[:count], refs[count], refs[-2], refs[-1]
    chip = lax.axis_index("ka") // CORES
    base = 0
    for at, step in enumerate(sizes):
        for gap in range(chips):
            start = base + lax.rem(chip - gap + chips, chips) * step
            rows = pl.ds(pl.multiple_of(start, SUBLANES), step)
            spot = pl.ds(gap * step, step)
            total = parts[at * group][:, spot, :]
            for part in parts[at * group + 1 : (at + 1) * group]:
                total = total + part[:, spot, :]
            collision[:, 0, rows, :] = total
            after[:, 0, rows, :] = less[:, 0, rows, :] + total
        base += chips * step


def call(kernel, out_shapes, in_specs, out_specs, args, scratch=(), after=(), limit=VMEM_LIMIT, aliases=None):
    count, skipped = len(args), len(after)

    def ordered(*refs):
        kernel(*refs[:count], *refs[count + skipped :])

    return pl.pallas_call(
        ordered,
        out_shape=out_shapes,
        in_specs=in_specs + [ANYWHERE] * skipped,
        out_specs=out_specs,
        scratch_shapes=scratch,
        input_output_aliases=aliases or {},
        cost_estimate=pl.CostEstimate(flops=1, bytes_accessed=1, transcendentals=0),
        compiler_params=pltpu.CompilerParams(vmem_limit_bytes=limit),
    )(*args, *after)


def body(green_less, green_great, screened):
    momenta, row_parts, col_parts = lax.axis_size("ka"), lax.axis_size("tr"), lax.axis_size("tc")
    member = lax.axis_index("tc") % (col_parts // row_parts)
    rows, cols = green_less.shape[2], green_less.shape[3]
    group, chips = col_parts // row_parts, momenta // CORES
    sizes = chunk_sizes(rows // chips // SUBLANES)
    bases = [chips * sum(sizes[:at]) for at in range(len(sizes))]
    f32 = functools.partial(jax.ShapeDtypeStruct, dtype=jnp.float32)
    bf16 = functools.partial(jax.ShapeDtypeStruct, dtype=jnp.bfloat16)
    inputs = (green_less, green_great, screened)
    scale = momenta**-1.5 * (rows * row_parts) ** -0.5
    tables = jnp.asarray(angle_tables(momenta))

    def to_chip(value, gap):
        moves = [
            (chip * CORES + core, (chip + gap) % chips * CORES + core) for chip in range(chips) for core in range(CORES)
        ]
        return lax.ppermute(value, "ka", moves)

    def to_core(value):
        return lax.ppermute(value, "ka", [(s, s + 1 - 2 * (s % CORES)) for s in range(momenta)])

    def to_panel(value, rows_on, cols_on):
        moves = []
        for i in range(row_parts):
            for j in range(col_parts):
                column = j // group * group + (j + cols_on) % group
                moves.append((i * col_parts + j, (i + rows_on) % row_parts * col_parts + column))
        return lax.ppermute(value, ("tr", "tc"), moves)

    def to_half(value, gap):
        return lax.ppermute(value, "tc", [(j, (j + group * gap) % col_parts) for j in range(col_parts)])

    def pack(at, passed, after):
        step, count = sizes[at], len(passed)
        outs = call(
            functools.partial(pack_kernel, chips, bases[at], step, count),
            [f32(value.shape) for value in passed] + [f32((3, 2, step, cols))] * chips,
            [IN_HBM] * 3 + [ANYWHERE] * count,
            [ANYWHERE] * count + [ANYWHERE if at else IN_VMEM] * chips,
            (*inputs, *passed),
            [pltpu.SemaphoreType.DMA((3 * chips,))],
            after,
            FIRST_LIMIT if at == 0 else VMEM_LIMIT,
            {3 + spot: spot for spot in range(count)},
        )
        return outs[count:], outs[:count]

    def gate(passed, after):
        count = len(passed)
        return call(
            lambda *refs: None,
            [f32(value.shape) for value in passed],
            [ANYWHERE] * count,
            [ANYWHERE] * count,
            passed,
            (),
            after,
            aliases={spot: spot for spot in range(count)},
        )

    def forward(pieces):
        return [to_chip(pieces[gap], -gap) for gap in range(1, chips)], to_core(pieces[0])

    def energy(at, here, other, after):
        return call(
            functools.partial(energy_kernel, chips, scale),
            [f32((2, sizes[at], cols))] * chips,
            [IN_SMEM] + [IN_VMEM] * momenta,
            [IN_VMEM] * chips,
            (tables, *here, *other),
            (),
            after,
        )

    def product(at, lefts, after):
        outs = call(
            functools.partial(product_kernel, row_parts, group, chips),
            [f32((2, chips * sizes[at], cols))] * group,
            [IN_VMEM] * (len(lefts) + 2),
            [IN_VMEM] * group,
            (*lefts, *right),
            (),
            after,
        )
        return [outs[0]] + [to_panel(outs[gap], 0, -gap) for gap in range(1, group)]

    pieces = [pack(0, (), ())[0]]
    sent = [forward(pieces[0])]

    blocks = green_less[:, 0].reshape(2, group, cols, cols)
    panels = []
    for rows_on in range(row_parts):
        for cols_on in range(group):
            block = lax.dynamic_index_in_dim(blocks, (member + cols_on) % group, 1, False)
            panels.append(to_panel(block, rows_on, cols_on) if rows_on + cols_on else block)
    extent = 2 * row_parts * cols

    lefts, results, last, arrived, returned = [], [], (), (), ()
    for at in range(len(sizes) + 1):
        if at < len(sizes):
            across, beside = sent[at]
            if at + 1 < len(sizes):
                fresh, across = pack(at + 1, across, (*arrived, *last))
                pieces.append(fresh)
                sent.append(forward(fresh))
            else:
                across = gate(across, (*arrived, *last, *(results[-2][1:] if len(results) > 1 else ())))
            gates = panels[1:group]
            if at == 1:
                right = call(
                    functools.partial(right_kernel, row_parts, group),
                    [bf16((extent, 2 * group * cols))] * 2,
                    [IN_VMEM] * len(panels),
                    [IN_VMEM] * 2,
                    panels,
                    (),
                    across,
                )
                gates = right
            here = [pieces[at][0], *across]
            other = [beside, *(to_core(piece) for piece in across)]
            sigmas = energy(at, here, other, gates)
            owned = [sigmas[0]] + [to_chip(sigmas[gap], gap) for gap in range(1, chips)]
            lefts.append([part for own in owned for part in [own] + [to_half(own, gap) for gap in range(1, row_parts)]])
            returned = owned[1:2]
            arrived = (*returned, *lefts[at][1:2])
            if at == 0:
                arrived += tuple(panels[group:])
            last = sigmas[:1]
        if at >= 1:
            before = results[-2][1:] if len(results) > 1 else ()
            gates = (*last, *(returned if at + 1 == len(sizes) else ()), *before)
            results.append(product(at - 1, lefts[at - 1], gates))
            last, returned = results[-1][:1], ()

    return call(
        functools.partial(final_kernel, group, chips, sizes),
        [f32(green_less.shape)] * 2,
        [IN_VMEM] * (len(sizes) * group + 1),
        [IN_VMEM] * 2,
        (*[part for result in results for part in result], green_less),
    )


def solution(mesh):
    spec = P(None, "ka", "tr", "tc")
    return jax.shard_map(body, mesh=mesh, in_specs=(spec,) * 3, out_specs=(spec,) * 2, check_vma=False)
```

```python
import functools
import math

import jax
import jax.numpy as jnp
import numpy as np
from jax import lax
from jax.experimental import pallas as pl
from jax.experimental.pallas import tpu as pltpu
from jax.sharding import PartitionSpec as P

CORES = 2
WEIGHTS = (8, 11, 8, 5)
SUBLANES, LANES = 8, 128
VMEM_LIMIT = 40 * 2**20
FIRST_LIMIT = 56 * 2**20
ANYWHERE = pl.BlockSpec(memory_space=pl.ANY)
IN_VMEM = pl.BlockSpec(memory_space=pltpu.VMEM)
IN_HBM = pl.BlockSpec(memory_space=pltpu.HBM)
IN_SMEM = pl.BlockSpec(memory_space=pltpu.SMEM)


def chunk_sizes(units):
    if units % sum(WEIGHTS):
        return [SUBLANES * part for part in (units // 2, units - units // 2) if part]
    return [SUBLANES * weight * units // sum(WEIGHTS) for weight in WEIGHTS]


def angle_tables(points):
    cosine = [[1.0, 0.0, -1.0, 0.0][4 * r // points] if 4 * r % points == 0 else math.cos(2 * math.pi * r / points) for r in range(points)]
    sine = [[0.0, 1.0, 0.0, -1.0][4 * r // points] if 4 * r % points == 0 else math.sin(2 * math.pi * r / points) for r in range(points)]
    return np.array([cosine, sine], np.float32)


def times_i(value, power):
    real, imag = value
    return [(real, imag), (-imag, real), (-real, -imag), (imag, -real)][power % 4]


def add(left, right):
    return (left[0] + right[0], left[1] + right[1])


def subtract(left, right):
    return (left[0] - right[0], left[1] - right[1])


def twiddle(value, index, points, sign):
    if 4 * index % points == 0:
        return times_i(value, sign * (4 * index // points))
    angle = sign * 2.0 * math.pi * index / points
    cosine, sine = math.cos(angle), math.sin(angle)
    real, imag = value
    return (real * cosine - imag * sine, imag * cosine + real * sine)


def transform(values, sign):
    points = len(values)
    if points == 1:
        return values
    if points % 2:
        return [
            functools.reduce(add, [twiddle(value, at * out % points, points, sign) for at, value in enumerate(values)])
            for out in range(points)
        ]
    even, odd = transform(values[::2], sign), transform(values[1::2], sign)
    odd = [twiddle(value, at, points, sign) for at, value in enumerate(odd)]
    return [add(e, o) for e, o in zip(even, odd)] + [subtract(e, o) for e, o in zip(even, odd)]


def at_rows(ref, start, size):
    return ref.at[:, 0, pl.ds(pl.multiple_of(start, SUBLANES), size), :]


def pack_kernel(chips, base, step, passed, *refs):
    sources, pieces, sem = refs[:3], refs[3 + 2 * passed : -1], refs[-1]
    chip = lax.axis_index("ka") // CORES
    copies = []
    for gap, piece in enumerate(pieces):
        start = base + lax.rem(chip - gap + chips, chips) * step
        for at, source in enumerate(sources):
            copies.append(pltpu.make_async_copy(at_rows(source, start, step), piece.at[at], sem.at[len(copies)]))
    for copy in copies:
        copy.start()
    for copy in copies:
        copy.wait()


def rotate(value, cosine, sine):
    return (value[0] * cosine - value[1] * sine, value[1] * cosine + value[0] * sine)


def energy_kernel(chips, scale, tables, *refs):
    here, other, sigmas = refs[:chips], refs[chips : 2 * chips], refs[2 * chips :]
    points = chips * CORES
    own = lax.axis_index("ka")
    side = (1 - 2 * lax.rem(own, CORES)).astype(jnp.float32)
    cosines = [tables[0, lax.rem(own * r, points)] for r in range(points)]
    sines = [tables[1, lax.rem(own * r, points)] for r in range(points)]
    step, across = here[0].shape[2], here[0].shape[3] // LANES
    root = points**-0.5

    def join(first, second):
        out = []
        for r in range(points):
            left, right = first[r % chips], second[r % chips]
            if 2 * r % points == 0:
                out.append(add(left, right) if r == 0 else subtract(left, right))
            elif 4 * r % points == 0:
                turned = (-right[1] * side, right[0] * side)
                out.append(add(left, turned) if 4 * r == points else subtract(left, turned))
            else:
                angle = 2.0 * math.pi * r / points
                out.append(add(left, rotate(right, math.cos(angle), math.sin(angle) * side)))
        return out

    def tile(index, carry):
        spot = (
            pl.ds(pl.multiple_of(lax.div(index, across) * SUBLANES, SUBLANES), SUBLANES),
            pl.ds(pl.multiple_of(lax.rem(index, across) * LANES, LANES), LANES),
        )
        lesser, greater, screen = (
            join(*(transform([(ref[at, 0, *spot], ref[at, 1, *spot]) for ref in group], 1) for group in (here, other)))
            for at in range(3)
        )
        values = []
        for r in range(points):
            less, great = lesser[r], greater[r]
            inter = screen[r] if r == 0 else rotate(screen[r], cosines[r], sines[r])
            polar_real = less[0] * great[1] - less[1] * great[0]
            polar_imag = less[0] * great[0] + less[1] * great[1]
            inter_real = inter[0] + polar_real * root
            inter_imag = inter[1] + polar_imag * root
            values.append(
                (
                    (less[0] * inter_imag + less[1] * inter_real) * -scale,
                    (less[0] * inter_real - less[1] * inter_imag) * scale,
                )
            )
        folded = [add(values[r], values[r + chips]) for r in range(chips)]
        for out, (real, imag) in zip(sigmas, transform(folded, -1)):
            out[0, *spot] = real
            out[1, *spot] = imag
        return carry

    lax.fori_loop(0, step // SUBLANES * across, tile, 0)


def split(value):
    high = value.astype(jnp.bfloat16)
    return high, (value - high.astype(jnp.float32)).astype(jnp.bfloat16)


def right_kernel(row_parts, group, *refs):
    pieces, high, low = refs[: row_parts * group], refs[-2], refs[-1]
    row_at, half = lax.axis_index("tr"), lax.axis_index("tc") // group
    depth, cols = pieces[0].shape[1:]
    for part in range(row_parts):
        place = lax.rem(half - row_at + part + row_parts, row_parts) * depth
        upper = pl.ds(pl.multiple_of(place, depth), depth)
        lower = pl.ds(pl.multiple_of(place + row_parts * depth, depth), depth)
        for gap in range(group):
            piece = pieces[part * group + gap]
            first = pl.ds(gap * cols, cols)
            second = pl.ds((group + gap) * cols, cols)
            real, imag = split(piece[0]), split(piece[1])
            for out, real_part, imag_part in zip((high, low), real, imag):
                out[upper, first] = real_part
                out[lower, second] = real_part
                out[upper, second] = imag_part
                out[lower, first] = -imag_part


def product_kernel(row_parts, group, chips, *refs):
    count = row_parts * chips
    sides, high, low, outs = refs[:count], refs[count], refs[count + 1], refs[count + 2 :]
    left = jnp.concatenate(
        [
            jnp.concatenate([sides[gap * row_parts + part][at] for at in (0, 1) for part in range(row_parts)], axis=1)
            for gap in range(chips)
        ],
        axis=0,
    )
    left_high, left_low = split(left)
    cols = outs[0].shape[-1]
    for at in range(2):
        for gap in range(group):
            spot = pl.ds((at * group + gap) * cols, cols)
            right_high, right_low = high[:, spot], low[:, spot]
            dot = functools.partial(jnp.dot, preferred_element_type=jnp.float32)
            outs[gap][at] = dot(left_high, right_high) + (dot(left_high, right_low) + dot(left_low, right_high))


def final_kernel(group, chips, sizes, *refs):
    count = len(sizes) * group
    parts, less, collision, after = refs[:count], refs[count], refs[-2], refs[-1]
    chip = lax.axis_index("ka") // CORES
    base = 0
    for at, step in enumerate(sizes):
        for gap in range(chips):
            start = base + lax.rem(chip - gap + chips, chips) * step
            rows = pl.ds(pl.multiple_of(start, SUBLANES), step)
            spot = pl.ds(gap * step, step)
            total = parts[at * group][:, spot, :]
            for part in parts[at * group + 1 : (at + 1) * group]:
                total = total + part[:, spot, :]
            collision[:, 0, rows, :] = total
            after[:, 0, rows, :] = less[:, 0, rows, :] + total
        base += chips * step


def call(kernel, out_shapes, in_specs, out_specs, args, scratch=(), after=(), limit=VMEM_LIMIT, aliases=None):
    count, skipped = len(args), len(after)

    def ordered(*refs):
        kernel(*refs[:count], *refs[count + skipped :])

    return pl.pallas_call(
        ordered,
        out_shape=out_shapes,
        in_specs=in_specs + [ANYWHERE] * skipped,
        out_specs=out_specs,
        scratch_shapes=scratch,
        input_output_aliases=aliases or {},
        cost_estimate=pl.CostEstimate(flops=1, bytes_accessed=1, transcendentals=0),
        compiler_params=pltpu.CompilerParams(vmem_limit_bytes=limit),
    )(*args, *after)


def body(green_less, green_great, screened):
    momenta, row_parts, col_parts = lax.axis_size("ka"), lax.axis_size("tr"), lax.axis_size("tc")
    member = lax.axis_index("tc") % (col_parts // row_parts)
    rows, cols = green_less.shape[2], green_less.shape[3]
    group, chips = col_parts // row_parts, momenta // CORES
    sizes = chunk_sizes(rows // chips // SUBLANES)
    bases = [chips * sum(sizes[:at]) for at in range(len(sizes))]
    f32 = functools.partial(jax.ShapeDtypeStruct, dtype=jnp.float32)
    bf16 = functools.partial(jax.ShapeDtypeStruct, dtype=jnp.bfloat16)
    inputs = (green_less, green_great, screened)
    scale = momenta**-1.5 * (rows * row_parts) ** -0.5
    tables = jnp.asarray(angle_tables(momenta))

    def to_chip(value, gap):
        moves = [
            (chip * CORES + core, (chip + gap) % chips * CORES + core) for chip in range(chips) for core in range(CORES)
        ]
        return lax.ppermute(value, "ka", moves)

    def to_core(value):
        return lax.ppermute(value, "ka", [(s, s + 1 - 2 * (s % CORES)) for s in range(momenta)])

    def to_panel(value, rows_on, cols_on):
        moves = []
        for i in range(row_parts):
            for j in range(col_parts):
                column = j // group * group + (j + cols_on) % group
                moves.append((i * col_parts + j, (i + rows_on) % row_parts * col_parts + column))
        return lax.ppermute(value, ("tr", "tc"), moves)

    def to_half(value, gap):
        return lax.ppermute(value, "tc", [(j, (j + group * gap) % col_parts) for j in range(col_parts)])

    def pack(at, passed, after):
        step, count = sizes[at], len(passed)
        outs = call(
            functools.partial(pack_kernel, chips, bases[at], step, count),
            [f32(value.shape) for value in passed] + [f32((3, 2, step, cols))] * chips,
            [IN_HBM] * 3 + [ANYWHERE] * count,
            [ANYWHERE] * count + [ANYWHERE if at else IN_VMEM] * chips,
            (*inputs, *passed),
            [pltpu.SemaphoreType.DMA((3 * chips,))],
            after,
            FIRST_LIMIT if at == 0 else VMEM_LIMIT,
            {3 + spot: spot for spot in range(count)},
        )
        return outs[count:], outs[:count]

    def gate(passed, after):
        count = len(passed)
        return call(
            lambda *refs: None,
            [f32(value.shape) for value in passed],
            [ANYWHERE] * count,
            [ANYWHERE] * count,
            passed,
            (),
            after,
            aliases={spot: spot for spot in range(count)},
        )

    def forward(pieces):
        return [to_chip(pieces[gap], -gap) for gap in range(1, chips)], to_core(pieces[0])

    def energy(at, here, other, after):
        return call(
            functools.partial(energy_kernel, chips, scale),
            [f32((2, sizes[at], cols))] * chips,
            [IN_SMEM] + [IN_VMEM] * momenta,
            [IN_VMEM] * chips,
            (tables, *here, *other),
            (),
            after,
        )

    def product(at, lefts, after):
        outs = call(
            functools.partial(product_kernel, row_parts, group, chips),
            [f32((2, chips * sizes[at], cols))] * group,
            [IN_VMEM] * (len(lefts) + 2),
            [IN_VMEM] * group,
            (*lefts, *right),
            (),
            after,
        )
        return [outs[0]] + [to_panel(outs[gap], 0, -gap) for gap in range(1, group)]

    pieces = [pack(0, (), ())[0]]
    sent = [forward(pieces[0])]

    blocks = green_less[:, 0].reshape(2, group, cols, cols)
    panels = []
    for rows_on in range(row_parts):
        for cols_on in range(group):
            block = lax.dynamic_index_in_dim(blocks, (member + cols_on) % group, 1, False)
            panels.append(to_panel(block, rows_on, cols_on) if rows_on + cols_on else block)
    extent = 2 * row_parts * cols

    lefts, results, last, arrived, returned = [], [], (), (), ()
    for at in range(len(sizes) + 1):
        if at < len(sizes):
            across, beside = sent[at]
            if at + 1 < len(sizes):
                fresh, across = pack(at + 1, across, (*arrived, *last))
                pieces.append(fresh)
                sent.append(forward(fresh))
            else:
                across = gate(across, (*arrived, *last, *(results[-2][1:] if len(results) > 1 else ())))
            gates = panels[1:group]
            if at == 1:
                right = call(
                    functools.partial(right_kernel, row_parts, group),
                    [bf16((extent, 2 * group * cols))] * 2,
                    [IN_VMEM] * len(panels),
                    [IN_VMEM] * 2,
                    panels,
                    (),
                    across,
                )
                gates = right
            here = [pieces[at][0], *across]
            other = [beside, *(to_core(piece) for piece in across)]
            sigmas = energy(at, here, other, gates)
            owned = [sigmas[0]] + [to_chip(sigmas[gap], gap) for gap in range(1, chips)]
            lefts.append([part for own in owned for part in [own] + [to_half(own, gap) for gap in range(1, row_parts)]])
            returned = owned[1:2]
            arrived = (*returned, *lefts[at][1:2])
            if at == 0:
                arrived += tuple(panels[group:])
            last = sigmas[:1]
        if at >= 1:
            before = results[-2][1:] if len(results) > 1 else ()
            gates = (*last, *(returned if at + 1 == len(sizes) else ()), *before)
            results.append(product(at - 1, lefts[at - 1], gates))
            last, returned = results[-1][:1], ()

    return call(
        functools.partial(final_kernel, group, chips, sizes),
        [f32(green_less.shape)] * 2,
        [IN_VMEM] * (len(sizes) * group + 1),
        [IN_VMEM] * 2,
        (*[part for result in results for part in result], green_less),
    )


def solution(mesh):
    spec = P(None, "ka", "tr", "tc")
    return jax.shard_map(body, mesh=mesh, in_specs=(spec,) * 3, out_specs=(spec,) * 2, check_vma=False)
```

```python
import functools
import math

import jax
import jax.numpy as jnp
import numpy as np
from jax import lax
from jax.experimental import pallas as pl
from jax.experimental.pallas import tpu as pltpu
from jax.sharding import PartitionSpec as P

CORES = 2
WEIGHTS = (8, 11, 8, 5)
SUBLANES, LANES = 8, 128
VMEM_LIMIT = 40 * 2**20
FIRST_LIMIT = 56 * 2**20
ANYWHERE = pl.BlockSpec(memory_space=pl.ANY)
IN_VMEM = pl.BlockSpec(memory_space=pltpu.VMEM)
IN_HBM = pl.BlockSpec(memory_space=pltpu.HBM)
IN_SMEM = pl.BlockSpec(memory_space=pltpu.SMEM)


def chunk_sizes(units):
    if units % sum(WEIGHTS):
        return [SUBLANES * part for part in (units // 2, units - units // 2) if part]
    return [SUBLANES * weight * units // sum(WEIGHTS) for weight in WEIGHTS]


def angle_tables(points):
    cosine = [[1.0, 0.0, -1.0, 0.0][4 * r // points] if 4 * r % points == 0 else math.cos(2 * math.pi * r / points) for r in range(points)]
    sine = [[0.0, 1.0, 0.0, -1.0][4 * r // points] if 4 * r % points == 0 else math.sin(2 * math.pi * r / points) for r in range(points)]
    return np.array([cosine, sine], np.float32)


def times_i(value, power):
    real, imag = value
    return [(real, imag), (-imag, real), (-real, -imag), (imag, -real)][power % 4]


def add(left, right):
    return (left[0] + right[0], left[1] + right[1])


def subtract(left, right):
    return (left[0] - right[0], left[1] - right[1])


def twiddle(value, index, points, sign):
    if 4 * index % points == 0:
        return times_i(value, sign * (4 * index // points))
    angle = sign * 2.0 * math.pi * index / points
    cosine, sine = math.cos(angle), math.sin(angle)
    real, imag = value
    return (real * cosine - imag * sine, imag * cosine + real * sine)


def transform(values, sign):
    points = len(values)
    if points == 1:
        return values
    if points % 2:
        return [
            functools.reduce(add, [twiddle(value, at * out % points, points, sign) for at, value in enumerate(values)])
            for out in range(points)
        ]
    even, odd = transform(values[::2], sign), transform(values[1::2], sign)
    odd = [twiddle(value, at, points, sign) for at, value in enumerate(odd)]
    return [add(e, o) for e, o in zip(even, odd)] + [subtract(e, o) for e, o in zip(even, odd)]


def at_rows(ref, start, size):
    return ref.at[:, 0, pl.ds(pl.multiple_of(start, SUBLANES), size), :]


def pack_kernel(chips, base, step, passed, *refs):
    sources, pieces, sem = refs[:3], refs[3 + 2 * passed : -1], refs[-1]
    chip = lax.axis_index("ka") // CORES
    copies = []
    for gap, piece in enumerate(pieces):
        start = base + lax.rem(chip - gap + chips, chips) * step
        for at, source in enumerate(sources):
            copies.append(pltpu.make_async_copy(at_rows(source, start, step), piece.at[at], sem.at[len(copies)]))
    for copy in copies:
        copy.start()
    for copy in copies:
        copy.wait()


def rotate(value, cosine, sine):
    return (value[0] * cosine - value[1] * sine, value[1] * cosine + value[0] * sine)


def energy_kernel(chips, scale, tables, *refs):
    here, other, sigmas = refs[:chips], refs[chips : 2 * chips], refs[2 * chips :]
    points = chips * CORES
    own = lax.axis_index("ka")
    side = (1 - 2 * lax.rem(own, CORES)).astype(jnp.float32)
    cosines = [tables[0, lax.rem(own * r, points)] for r in range(points)]
    sines = [tables[1, lax.rem(own * r, points)] for r in range(points)]
    step, across = here[0].shape[2], here[0].shape[3] // LANES
    root = points**-0.5

    def join(first, second):
        out = []
        for r in range(points):
            left, right = first[r % chips], second[r % chips]
            if 2 * r % points == 0:
                out.append(add(left, right) if r == 0 else subtract(left, right))
            elif 4 * r % points == 0:
                turned = (-right[1] * side, right[0] * side)
                out.append(add(left, turned) if 4 * r == points else subtract(left, turned))
            else:
                angle = 2.0 * math.pi * r / points
                out.append(add(left, rotate(right, math.cos(angle), math.sin(angle) * side)))
        return out

    def tile(index, carry):
        spot = (
            pl.ds(pl.multiple_of(lax.div(index, across) * SUBLANES, SUBLANES), SUBLANES),
            pl.ds(pl.multiple_of(lax.rem(index, across) * LANES, LANES), LANES),
        )
        lesser, greater, screen = (
            join(*(transform([(ref[at, 0, *spot], ref[at, 1, *spot]) for ref in group], 1) for group in (here, other)))
            for at in range(3)
        )
        values = []
        for r in range(points):
            less, great = lesser[r], greater[r]
            inter = screen[r] if r == 0 else rotate(screen[r], cosines[r], sines[r])
            polar_real = less[0] * great[1] - less[1] * great[0]
            polar_imag = less[0] * great[0] + less[1] * great[1]
            inter_real = inter[0] + polar_real * root
            inter_imag = inter[1] + polar_imag * root
            values.append(
                (
                    (less[0] * inter_imag + less[1] * inter_real) * -scale,
                    (less[0] * inter_real - less[1] * inter_imag) * scale,
                )
            )
        folded = [add(values[r], values[r + chips]) for r in range(chips)]
        for out, (real, imag) in zip(sigmas, transform(folded, -1)):
            out[0, *spot] = real
            out[1, *spot] = imag
        return carry

    lax.fori_loop(0, step // SUBLANES * across, tile, 0)


def split(value):
    high = value.astype(jnp.bfloat16)
    return high, (value - high.astype(jnp.float32)).astype(jnp.bfloat16)


def right_kernel(row_parts, group, *refs):
    pieces, high, low = refs[: row_parts * group], refs[-2], refs[-1]
    row_at, half = lax.axis_index("tr"), lax.axis_index("tc") // group
    depth, cols = pieces[0].shape[1:]
    for part in range(row_parts):
        place = lax.rem(half - row_at + part + row_parts, row_parts) * depth
        upper = pl.ds(pl.multiple_of(place, depth), depth)
        lower = pl.ds(pl.multiple_of(place + row_parts * depth, depth), depth)
        for gap in range(group):
            piece = pieces[part * group + gap]
            first = pl.ds(gap * cols, cols)
            second = pl.ds((group + gap) * cols, cols)
            real, imag = split(piece[0]), split(piece[1])
            for out, real_part, imag_part in zip((high, low), real, imag):
                out[upper, first] = real_part
                out[lower, second] = real_part
                out[upper, second] = imag_part
                out[lower, first] = -imag_part


def product_kernel(row_parts, group, chips, *refs):
    count = row_parts * chips
    sides, high, low, outs = refs[:count], refs[count], refs[count + 1], refs[count + 2 :]
    left = jnp.concatenate(
        [
            jnp.concatenate([sides[gap * row_parts + part][at] for at in (0, 1) for part in range(row_parts)], axis=1)
            for gap in range(chips)
        ],
        axis=0,
    )
    left_high, left_low = split(left)
    cols = outs[0].shape[-1]
    for at in range(2):
        for gap in range(group):
            spot = pl.ds((at * group + gap) * cols, cols)
            right_high, right_low = high[:, spot], low[:, spot]
            dot = functools.partial(jnp.dot, preferred_element_type=jnp.float32)
            outs[gap][at] = dot(left_high, right_high) + (dot(left_high, right_low) + dot(left_low, right_high))


def final_kernel(group, chips, sizes, *refs):
    count = len(sizes) * group
    parts, less, collision, after = refs[:count], refs[count], refs[-2], refs[-1]
    chip = lax.axis_index("ka") // CORES
    base = 0
    for at, step in enumerate(sizes):
        for gap in range(chips):
            start = base + lax.rem(chip - gap + chips, chips) * step
            rows = pl.ds(pl.multiple_of(start, SUBLANES), step)
            spot = pl.ds(gap * step, step)
            total = parts[at * group][:, spot, :]
            for part in parts[at * group + 1 : (at + 1) * group]:
                total = total + part[:, spot, :]
            collision[:, 0, rows, :] = total
            after[:, 0, rows, :] = less[:, 0, rows, :] + total
        base += chips * step


def call(kernel, out_shapes, in_specs, out_specs, args, scratch=(), after=(), limit=VMEM_LIMIT, aliases=None):
    count, skipped = len(args), len(after)

    def ordered(*refs):
        kernel(*refs[:count], *refs[count + skipped :])

    return pl.pallas_call(
        ordered,
        out_shape=out_shapes,
        in_specs=in_specs + [ANYWHERE] * skipped,
        out_specs=out_specs,
        scratch_shapes=scratch,
        input_output_aliases=aliases or {},
        cost_estimate=pl.CostEstimate(flops=1, bytes_accessed=1, transcendentals=0),
        compiler_params=pltpu.CompilerParams(vmem_limit_bytes=limit),
    )(*args, *after)


def body(green_less, green_great, screened):
    momenta, row_parts, col_parts = lax.axis_size("ka"), lax.axis_size("tr"), lax.axis_size("tc")
    member = lax.axis_index("tc") % (col_parts // row_parts)
    rows, cols = green_less.shape[2], green_less.shape[3]
    group, chips = col_parts // row_parts, momenta // CORES
    sizes = chunk_sizes(rows // chips // SUBLANES)
    bases = [chips * sum(sizes[:at]) for at in range(len(sizes))]
    f32 = functools.partial(jax.ShapeDtypeStruct, dtype=jnp.float32)
    bf16 = functools.partial(jax.ShapeDtypeStruct, dtype=jnp.bfloat16)
    inputs = (green_less, green_great, screened)
    scale = momenta**-1.5 * (rows * row_parts) ** -0.5
    tables = jnp.asarray(angle_tables(momenta))

    def to_chip(value, gap):
        moves = [
            (chip * CORES + core, (chip + gap) % chips * CORES + core) for chip in range(chips) for core in range(CORES)
        ]
        return lax.ppermute(value, "ka", moves)

    def to_core(value):
        return lax.ppermute(value, "ka", [(s, s + 1 - 2 * (s % CORES)) for s in range(momenta)])

    def to_panel(value, rows_on, cols_on):
        moves = []
        for i in range(row_parts):
            for j in range(col_parts):
                column = j // group * group + (j + cols_on) % group
                moves.append((i * col_parts + j, (i + rows_on) % row_parts * col_parts + column))
        return lax.ppermute(value, ("tr", "tc"), moves)

    def to_half(value, gap):
        return lax.ppermute(value, "tc", [(j, (j + group * gap) % col_parts) for j in range(col_parts)])

    def pack(at, passed, after):
        step, count = sizes[at], len(passed)
        outs = call(
            functools.partial(pack_kernel, chips, bases[at], step, count),
            [f32(value.shape) for value in passed] + [f32((3, 2, step, cols))] * chips,
            [IN_HBM] * 3 + [ANYWHERE] * count,
            [ANYWHERE] * count + [ANYWHERE if at else IN_VMEM] * chips,
            (*inputs, *passed),
            [pltpu.SemaphoreType.DMA((3 * chips,))],
            after,
            FIRST_LIMIT if at == 0 else VMEM_LIMIT,
            {3 + spot: spot for spot in range(count)},
        )
        return outs[count:], outs[:count]

    def gate(passed, after):
        count = len(passed)
        return call(
            lambda *refs: None,
            [f32(value.shape) for value in passed],
            [ANYWHERE] * count,
            [ANYWHERE] * count,
            passed,
            (),
            after,
            aliases={spot: spot for spot in range(count)},
        )

    def forward(pieces):
        return [to_chip(pieces[gap], -gap) for gap in range(1, chips)], to_core(pieces[0])

    def energy(at, here, other, after):
        return call(
            functools.partial(energy_kernel, chips, scale),
            [f32((2, sizes[at], cols))] * chips,
            [IN_SMEM] + [IN_VMEM] * momenta,
            [IN_VMEM] * chips,
            (tables, *here, *other),
            (),
            after,
        )

    def product(at, lefts, after):
        outs = call(
            functools.partial(product_kernel, row_parts, group, chips),
            [f32((2, chips * sizes[at], cols))] * group,
            [IN_VMEM] * (len(lefts) + 2),
            [IN_VMEM] * group,
            (*lefts, *right),
            (),
            after,
        )
        return [outs[0]] + [to_panel(outs[gap], 0, -gap) for gap in range(1, group)]

    pieces = [pack(0, (), ())[0]]
    sent = [forward(pieces[0])]

    blocks = green_less[:, 0].reshape(2, group, cols, cols)
    panels = []
    for rows_on in range(row_parts):
        for cols_on in range(group):
            block = lax.dynamic_index_in_dim(blocks, (member + cols_on) % group, 1, False)
            panels.append(to_panel(block, rows_on, cols_on) if rows_on + cols_on else block)
    extent = 2 * row_parts * cols

    lefts, results, last, arrived, returned = [], [], (), (), ()
    for at in range(len(sizes) + 1):
        if at < len(sizes):
            across, beside = sent[at]
            if at + 1 < len(sizes):
                fresh, across = pack(at + 1, across, (*arrived, *last))
                pieces.append(fresh)
                sent.append(forward(fresh))
            else:
                across = gate(across, (*arrived, *last, *(results[-2][1:] if len(results) > 1 else ())))
            gates = () if at else panels[1 : group + 1]
            if at == 1:
                right = call(
                    functools.partial(right_kernel, row_parts, group),
                    [bf16((extent, 2 * group * cols))] * 2,
                    [IN_VMEM] * len(panels),
                    [IN_VMEM] * 2,
                    panels,
                    (),
                    across,
                )
                gates = right
            here = [pieces[at][0], *across]
            other = [beside, *(to_core(piece) for piece in across)]
            sigmas = energy(at, here, other, gates)
            owned = [sigmas[0]] + [to_chip(sigmas[gap], gap) for gap in range(1, chips)]
            lefts.append([part for own in owned for part in [own] + [to_half(own, gap) for gap in range(1, row_parts)]])
            returned = owned[1:2]
            arrived = (*returned, *lefts[at][1:2])
            if at == 0:
                arrived += tuple(panels[group + 1 :])
            last = sigmas[:1]
        if at >= 1:
            before = results[-2][1:] if len(results) > 1 else ()
            gates = (*last, *(returned if at + 1 == len(sizes) else ()), *before)
            results.append(product(at - 1, lefts[at - 1], gates))
            last, returned = results[-1][:1], ()

    return call(
        functools.partial(final_kernel, group, chips, sizes),
        [f32(green_less.shape)] * 2,
        [IN_VMEM] * (len(sizes) * group + 1),
        [IN_VMEM] * 2,
        (*[part for result in results for part in result], green_less),
    )


def solution(mesh):
    spec = P(None, "ka", "tr", "tc")
    return jax.shard_map(body, mesh=mesh, in_specs=(spec,) * 3, out_specs=(spec,) * 2, check_vma=False)
```

```python
import functools
import math

import jax
import jax.numpy as jnp
import numpy as np
from jax import lax
from jax.experimental import pallas as pl
from jax.experimental.pallas import tpu as pltpu
from jax.sharding import PartitionSpec as P

CORES = 2
WEIGHTS = (8, 11, 8, 5)
SUBLANES, LANES = 8, 128
VMEM_LIMIT = 40 * 2**20
FIRST_LIMIT = 56 * 2**20
ANYWHERE = pl.BlockSpec(memory_space=pl.ANY)
IN_VMEM = pl.BlockSpec(memory_space=pltpu.VMEM)
IN_HBM = pl.BlockSpec(memory_space=pltpu.HBM)
IN_SMEM = pl.BlockSpec(memory_space=pltpu.SMEM)


def chunk_sizes(units):
    if units % sum(WEIGHTS):
        return [SUBLANES * part for part in (units // 2, units - units // 2) if part]
    return [SUBLANES * weight * units // sum(WEIGHTS) for weight in WEIGHTS]


def angle_tables(points):
    cosine = [[1.0, 0.0, -1.0, 0.0][4 * r // points] if 4 * r % points == 0 else math.cos(2 * math.pi * r / points) for r in range(points)]
    sine = [[0.0, 1.0, 0.0, -1.0][4 * r // points] if 4 * r % points == 0 else math.sin(2 * math.pi * r / points) for r in range(points)]
    return np.array([cosine, sine], np.float32)


def times_i(value, power):
    real, imag = value
    return [(real, imag), (-imag, real), (-real, -imag), (imag, -real)][power % 4]


def add(left, right):
    return (left[0] + right[0], left[1] + right[1])


def subtract(left, right):
    return (left[0] - right[0], left[1] - right[1])


def twiddle(value, index, points, sign):
    if 4 * index % points == 0:
        return times_i(value, sign * (4 * index // points))
    angle = sign * 2.0 * math.pi * index / points
    cosine, sine = math.cos(angle), math.sin(angle)
    real, imag = value
    return (real * cosine - imag * sine, imag * cosine + real * sine)


def transform(values, sign):
    points = len(values)
    if points == 1:
        return values
    if points % 2:
        return [
            functools.reduce(add, [twiddle(value, at * out % points, points, sign) for at, value in enumerate(values)])
            for out in range(points)
        ]
    even, odd = transform(values[::2], sign), transform(values[1::2], sign)
    odd = [twiddle(value, at, points, sign) for at, value in enumerate(odd)]
    return [add(e, o) for e, o in zip(even, odd)] + [subtract(e, o) for e, o in zip(even, odd)]


def at_rows(ref, start, size):
    return ref.at[:, 0, pl.ds(pl.multiple_of(start, SUBLANES), size), :]


def pack_kernel(chips, base, step, passed, *refs):
    sources, pieces, sem = refs[:3], refs[3 + 2 * passed : -1], refs[-1]
    chip = lax.axis_index("ka") // CORES
    copies = []
    for gap, piece in enumerate(pieces):
        start = base + lax.rem(chip - gap + chips, chips) * step
        for at, source in enumerate(sources):
            copies.append(pltpu.make_async_copy(at_rows(source, start, step), piece.at[at], sem.at[len(copies)]))
    for copy in copies:
        copy.start()
    for copy in copies:
        copy.wait()


def rotate(value, cosine, sine):
    return (value[0] * cosine - value[1] * sine, value[1] * cosine + value[0] * sine)


def energy_kernel(chips, scale, tables, *refs):
    here, other, sigmas = refs[:chips], refs[chips : 2 * chips], refs[2 * chips :]
    points = chips * CORES
    own = lax.axis_index("ka")
    side = (1 - 2 * lax.rem(own, CORES)).astype(jnp.float32)
    cosines = [tables[0, lax.rem(own * r, points)] for r in range(points)]
    sines = [tables[1, lax.rem(own * r, points)] for r in range(points)]
    step, across = here[0].shape[2], here[0].shape[3] // LANES
    root = points**-0.5

    def join(first, second):
        out = []
        for r in range(points):
            left, right = first[r % chips], second[r % chips]
            if 2 * r % points == 0:
                out.append(add(left, right) if r == 0 else subtract(left, right))
            elif 4 * r % points == 0:
                turned = (-right[1] * side, right[0] * side)
                out.append(add(left, turned) if 4 * r == points else subtract(left, turned))
            else:
                angle = 2.0 * math.pi * r / points
                out.append(add(left, rotate(right, math.cos(angle), math.sin(angle) * side)))
        return out

    def tile(index, carry):
        spot = (
            pl.ds(pl.multiple_of(lax.div(index, across) * SUBLANES, SUBLANES), SUBLANES),
            pl.ds(pl.multiple_of(lax.rem(index, across) * LANES, LANES), LANES),
        )
        lesser, greater, screen = (
            join(*(transform([(ref[at, 0, *spot], ref[at, 1, *spot]) for ref in group], 1) for group in (here, other)))
            for at in range(3)
        )
        values = []
        for r in range(points):
            less, great = lesser[r], greater[r]
            inter = screen[r] if r == 0 else rotate(screen[r], cosines[r], sines[r])
            polar_real = less[0] * great[1] - less[1] * great[0]
            polar_imag = less[0] * great[0] + less[1] * great[1]
            inter_real = inter[0] + polar_real * root
            inter_imag = inter[1] + polar_imag * root
            values.append(
                (
                    (less[0] * inter_imag + less[1] * inter_real) * -scale,
                    (less[0] * inter_real - less[1] * inter_imag) * scale,
                )
            )
        folded = [add(values[r], values[r + chips]) for r in range(chips)]
        for out, (real, imag) in zip(sigmas, transform(folded, -1)):
            out[0, *spot] = real
            out[1, *spot] = imag
        return carry

    lax.fori_loop(0, step // SUBLANES * across, tile, 0)


def split(value):
    high = value.astype(jnp.bfloat16)
    return high, (value - high.astype(jnp.float32)).astype(jnp.bfloat16)


def right_kernel(row_parts, group, *refs):
    pieces, high, low = refs[: row_parts * group], refs[-2], refs[-1]
    row_at, half = lax.axis_index("tr"), lax.axis_index("tc") // group
    depth, cols = pieces[0].shape[1:]
    for part in range(row_parts):
        place = lax.rem(half - row_at + part + row_parts, row_parts) * depth
        upper = pl.ds(pl.multiple_of(place, depth), depth)
        lower = pl.ds(pl.multiple_of(place + row_parts * depth, depth), depth)
        for gap in range(group):
            piece = pieces[part * group + gap]
            first = pl.ds(gap * cols, cols)
            second = pl.ds((group + gap) * cols, cols)
            real, imag = split(piece[0]), split(piece[1])
            for out, real_part, imag_part in zip((high, low), real, imag):
                out[upper, first] = real_part
                out[lower, second] = real_part
                out[upper, second] = imag_part
                out[lower, first] = -imag_part


def product_kernel(row_parts, group, chips, *refs):
    count = row_parts * chips
    sides, high, low, outs = refs[:count], refs[count], refs[count + 1], refs[count + 2 :]
    left = jnp.concatenate(
        [
            jnp.concatenate([sides[gap * row_parts + part][at] for at in (0, 1) for part in range(row_parts)], axis=1)
            for gap in range(chips)
        ],
        axis=0,
    )
    left_high, left_low = split(left)
    cols = outs[0].shape[-1]
    for at in range(2):
        for gap in range(group):
            spot = pl.ds((at * group + gap) * cols, cols)
            right_high, right_low = high[:, spot], low[:, spot]
            dot = functools.partial(jnp.dot, preferred_element_type=jnp.float32)
            outs[gap][at] = dot(left_high, right_high) + (dot(left_high, right_low) + dot(left_low, right_high))


def final_kernel(group, chips, sizes, *refs):
    count = len(sizes) * group
    parts, less, collision, after = refs[:count], refs[count], refs[-2], refs[-1]
    chip = lax.axis_index("ka") // CORES
    base = 0
    for at, step in enumerate(sizes):
        for gap in range(chips):
            start = base + lax.rem(chip - gap + chips, chips) * step
            rows = pl.ds(pl.multiple_of(start, SUBLANES), step)
            spot = pl.ds(gap * step, step)
            total = parts[at * group][:, spot, :]
            for part in parts[at * group + 1 : (at + 1) * group]:
                total = total + part[:, spot, :]
            collision[:, 0, rows, :] = total
            after[:, 0, rows, :] = less[:, 0, rows, :] + total
        base += chips * step


def call(kernel, out_shapes, in_specs, out_specs, args, scratch=(), after=(), limit=VMEM_LIMIT, aliases=None):
    count, skipped = len(args), len(after)

    def ordered(*refs):
        kernel(*refs[:count], *refs[count + skipped :])

    return pl.pallas_call(
        ordered,
        out_shape=out_shapes,
        in_specs=in_specs + [ANYWHERE] * skipped,
        out_specs=out_specs,
        scratch_shapes=scratch,
        input_output_aliases=aliases or {},
        cost_estimate=pl.CostEstimate(flops=1, bytes_accessed=1, transcendentals=0),
        compiler_params=pltpu.CompilerParams(vmem_limit_bytes=limit),
    )(*args, *after)


def body(green_less, green_great, screened):
    momenta, row_parts, col_parts = lax.axis_size("ka"), lax.axis_size("tr"), lax.axis_size("tc")
    member = lax.axis_index("tc") % (col_parts // row_parts)
    rows, cols = green_less.shape[2], green_less.shape[3]
    group, chips = col_parts // row_parts, momenta // CORES
    sizes = chunk_sizes(rows // chips // SUBLANES)
    bases = [chips * sum(sizes[:at]) for at in range(len(sizes))]
    f32 = functools.partial(jax.ShapeDtypeStruct, dtype=jnp.float32)
    bf16 = functools.partial(jax.ShapeDtypeStruct, dtype=jnp.bfloat16)
    inputs = (green_less, green_great, screened)
    scale = momenta**-1.5 * (rows * row_parts) ** -0.5
    tables = jnp.asarray(angle_tables(momenta))

    def to_chip(value, gap):
        moves = [
            (chip * CORES + core, (chip + gap) % chips * CORES + core) for chip in range(chips) for core in range(CORES)
        ]
        return lax.ppermute(value, "ka", moves)

    def to_core(value):
        return lax.ppermute(value, "ka", [(s, s + 1 - 2 * (s % CORES)) for s in range(momenta)])

    def to_panel(value, rows_on, cols_on):
        moves = []
        for i in range(row_parts):
            for j in range(col_parts):
                column = j // group * group + (j + cols_on) % group
                moves.append((i * col_parts + j, (i + rows_on) % row_parts * col_parts + column))
        return lax.ppermute(value, ("tr", "tc"), moves)

    def to_half(value, gap):
        return lax.ppermute(value, "tc", [(j, (j + group * gap) % col_parts) for j in range(col_parts)])

    def pack(at, passed, after):
        step, count = sizes[at], len(passed)
        outs = call(
            functools.partial(pack_kernel, chips, bases[at], step, count),
            [f32(value.shape) for value in passed] + [f32((3, 2, step, cols))] * chips,
            [IN_HBM] * 3 + [ANYWHERE] * count,
            [ANYWHERE] * count + [ANYWHERE if at else IN_VMEM] * chips,
            (*inputs, *passed),
            [pltpu.SemaphoreType.DMA((3 * chips,))],
            after,
            FIRST_LIMIT if at == 0 else VMEM_LIMIT,
            {3 + spot: spot for spot in range(count)},
        )
        return outs[count:], outs[:count]

    def gate(passed, after):
        count = len(passed)
        return call(
            lambda *refs: None,
            [f32(value.shape) for value in passed],
            [ANYWHERE] * count,
            [ANYWHERE] * count,
            passed,
            (),
            after,
            aliases={spot: spot for spot in range(count)},
        )

    def forward(pieces):
        return [to_chip(pieces[gap], -gap) for gap in range(1, chips)], to_core(pieces[0])

    def energy(at, here, other, after):
        return call(
            functools.partial(energy_kernel, chips, scale),
            [f32((2, sizes[at], cols))] * chips,
            [IN_SMEM] + [IN_VMEM] * momenta,
            [IN_VMEM] * chips,
            (tables, *here, *other),
            (),
            after,
        )

    def product(at, lefts, after):
        outs = call(
            functools.partial(product_kernel, row_parts, group, chips),
            [f32((2, chips * sizes[at], cols))] * group,
            [IN_VMEM] * (len(lefts) + 2),
            [IN_VMEM] * group,
            (*lefts, *right),
            (),
            after,
        )
        return [outs[0]] + [to_panel(outs[gap], 0, -gap) for gap in range(1, group)]

    pieces = [pack(0, (), ())[0]]
    sent = [forward(pieces[0])]

    blocks = green_less[:, 0].reshape(2, group, cols, cols)
    panels = []
    for rows_on in range(row_parts):
        for cols_on in range(group):
            block = lax.dynamic_index_in_dim(blocks, (member + cols_on) % group, 1, False)
            panels.append(to_panel(block, rows_on, cols_on) if rows_on + cols_on else block)
    extent = 2 * row_parts * cols

    lefts, results, last, arrived, returned = [], [], (), (), ()
    for at in range(len(sizes) + 1):
        if at < len(sizes):
            across, beside = sent[at]
            if at + 1 < len(sizes):
                fresh, across = pack(at + 1, across, (*arrived, *last))
                pieces.append(fresh)
                sent.append(forward(fresh))
            else:
                across = gate(across, (*arrived, *last, *(results[-2][1:] if len(results) > 1 else ())))
            gates = () if at else panels[1 : group + 1]
            if at == 1:
                right = call(
                    functools.partial(right_kernel, row_parts, group),
                    [bf16((extent, 2 * group * cols))] * 2,
                    [IN_VMEM] * len(panels),
                    [IN_VMEM] * 2,
                    panels,
                    (),
                    across,
                )
                gates = right
            here = [pieces[at][0], *across]
            other = [beside, *(to_core(piece) for piece in across)]
            sigmas = energy(at, here, other, gates)
            owned = [sigmas[0]] + [to_chip(sigmas[gap], gap) for gap in range(1, chips)]
            lefts.append([part for own in owned for part in [own] + [to_half(own, gap) for gap in range(1, row_parts)]])
            returned = owned[1:2]
            arrived = (*returned, *lefts[at][1:2])
            if at == 0:
                arrived += tuple(panels[group + 1 :])
            last = sigmas[:1]
        if at >= 1:
            before = results[-2][1:] if len(results) > 1 else ()
            gates = (*last, *((*returned, *lefts[at][1:2]) if at + 1 == len(sizes) else ()), *before)
            results.append(product(at - 1, lefts[at - 1], gates))
            last, returned = results[-1][:1], ()

    return call(
        functools.partial(final_kernel, group, chips, sizes),
        [f32(green_less.shape)] * 2,
        [IN_VMEM] * (len(sizes) * group + 1),
        [IN_VMEM] * 2,
        (*[part for result in results for part in result], green_less),
    )


def solution(mesh):
    spec = P(None, "ka", "tr", "tc")
    return jax.shard_map(body, mesh=mesh, in_specs=(spec,) * 3, out_specs=(spec,) * 2, check_vma=False)
```

```python
import functools
import math

import jax
import jax.numpy as jnp
import numpy as np
from jax import lax
from jax.experimental import pallas as pl
from jax.experimental.pallas import tpu as pltpu
from jax.sharding import PartitionSpec as P

CORES = 2
WEIGHTS = (8, 11, 8, 5)
SUBLANES, LANES = 8, 128
VMEM_LIMIT = 40 * 2**20
FIRST_LIMIT = 56 * 2**20
ANYWHERE = pl.BlockSpec(memory_space=pl.ANY)
IN_VMEM = pl.BlockSpec(memory_space=pltpu.VMEM)
IN_HBM = pl.BlockSpec(memory_space=pltpu.HBM)
IN_SMEM = pl.BlockSpec(memory_space=pltpu.SMEM)


def chunk_sizes(units):
    if units % sum(WEIGHTS):
        return [SUBLANES * part for part in (units // 2, units - units // 2) if part]
    return [SUBLANES * weight * units // sum(WEIGHTS) for weight in WEIGHTS]


def angle_tables(points):
    cosine = [[1.0, 0.0, -1.0, 0.0][4 * r // points] if 4 * r % points == 0 else math.cos(2 * math.pi * r / points) for r in range(points)]
    sine = [[0.0, 1.0, 0.0, -1.0][4 * r // points] if 4 * r % points == 0 else math.sin(2 * math.pi * r / points) for r in range(points)]
    return np.array([cosine, sine], np.float32)


def times_i(value, power):
    real, imag = value
    return [(real, imag), (-imag, real), (-real, -imag), (imag, -real)][power % 4]


def add(left, right):
    return (left[0] + right[0], left[1] + right[1])


def subtract(left, right):
    return (left[0] - right[0], left[1] - right[1])


def twiddle(value, index, points, sign):
    if 4 * index % points == 0:
        return times_i(value, sign * (4 * index // points))
    angle = sign * 2.0 * math.pi * index / points
    cosine, sine = math.cos(angle), math.sin(angle)
    real, imag = value
    return (real * cosine - imag * sine, imag * cosine + real * sine)


def transform(values, sign):
    points = len(values)
    if points == 1:
        return values
    if points % 2:
        return [
            functools.reduce(add, [twiddle(value, at * out % points, points, sign) for at, value in enumerate(values)])
            for out in range(points)
        ]
    even, odd = transform(values[::2], sign), transform(values[1::2], sign)
    odd = [twiddle(value, at, points, sign) for at, value in enumerate(odd)]
    return [add(e, o) for e, o in zip(even, odd)] + [subtract(e, o) for e, o in zip(even, odd)]


def at_rows(ref, start, size):
    return ref.at[:, 0, pl.ds(pl.multiple_of(start, SUBLANES), size), :]


def pack_kernel(chips, base, step, passed, *refs):
    sources, pieces, sem = refs[:3], refs[3 + 2 * passed : -1], refs[-1]
    chip = lax.axis_index("ka") // CORES
    copies = []
    for gap, piece in enumerate(pieces):
        start = base + lax.rem(chip - gap + chips, chips) * step
        for at, source in enumerate(sources):
            copies.append(pltpu.make_async_copy(at_rows(source, start, step), piece.at[at], sem.at[len(copies)]))
    for copy in copies:
        copy.start()
    for copy in copies:
        copy.wait()


def rotate(value, cosine, sine):
    return (value[0] * cosine - value[1] * sine, value[1] * cosine + value[0] * sine)


def energy_kernel(chips, scale, tables, *refs):
    here, other, sigmas = refs[:chips], refs[chips : 2 * chips], refs[2 * chips :]
    points = chips * CORES
    own = lax.axis_index("ka")
    side = (1 - 2 * lax.rem(own, CORES)).astype(jnp.float32)
    cosines = [tables[0, lax.rem(own * r, points)] for r in range(points)]
    sines = [tables[1, lax.rem(own * r, points)] for r in range(points)]
    step, across = here[0].shape[2], here[0].shape[3] // LANES
    root = points**-0.5

    def join(first, second):
        out = []
        for r in range(points):
            left, right = first[r % chips], second[r % chips]
            if 2 * r % points == 0:
                out.append(add(left, right) if r == 0 else subtract(left, right))
            elif 4 * r % points == 0:
                turned = (-right[1] * side, right[0] * side)
                out.append(add(left, turned) if 4 * r == points else subtract(left, turned))
            else:
                angle = 2.0 * math.pi * r / points
                out.append(add(left, rotate(right, math.cos(angle), math.sin(angle) * side)))
        return out

    def tile(index, carry):
        spot = (
            pl.ds(pl.multiple_of(lax.div(index, across) * SUBLANES, SUBLANES), SUBLANES),
            pl.ds(pl.multiple_of(lax.rem(index, across) * LANES, LANES), LANES),
        )
        lesser, greater, screen = (
            join(*(transform([(ref[at, 0, *spot], ref[at, 1, *spot]) for ref in group], 1) for group in (here, other)))
            for at in range(3)
        )
        values = []
        for r in range(points):
            less, great = lesser[r], greater[r]
            inter = screen[r] if r == 0 else rotate(screen[r], cosines[r], sines[r])
            polar_real = less[0] * great[1] - less[1] * great[0]
            polar_imag = less[0] * great[0] + less[1] * great[1]
            inter_real = inter[0] + polar_real * root
            inter_imag = inter[1] + polar_imag * root
            values.append(
                (
                    (less[0] * inter_imag + less[1] * inter_real) * -scale,
                    (less[0] * inter_real - less[1] * inter_imag) * scale,
                )
            )
        folded = [add(values[r], values[r + chips]) for r in range(chips)]
        for out, (real, imag) in zip(sigmas, transform(folded, -1)):
            out[0, *spot] = real
            out[1, *spot] = imag
        return carry

    lax.fori_loop(0, step // SUBLANES * across, tile, 0)


def split(value):
    high = value.astype(jnp.bfloat16)
    return high, (value - high.astype(jnp.float32)).astype(jnp.bfloat16)


def right_kernel(row_parts, group, *refs):
    pieces, high, low = refs[: row_parts * group], refs[-2], refs[-1]
    row_at, half = lax.axis_index("tr"), lax.axis_index("tc") // group
    depth, cols = pieces[0].shape[1:]
    for part in range(row_parts):
        place = lax.rem(half - row_at + part + row_parts, row_parts) * depth
        upper = pl.ds(pl.multiple_of(place, depth), depth)
        lower = pl.ds(pl.multiple_of(place + row_parts * depth, depth), depth)
        for gap in range(group):
            piece = pieces[part * group + gap]
            first = pl.ds(gap * cols, cols)
            second = pl.ds((group + gap) * cols, cols)
            real, imag = split(piece[0]), split(piece[1])
            for out, real_part, imag_part in zip((high, low), real, imag):
                out[upper, first] = real_part
                out[lower, second] = real_part
                out[upper, second] = imag_part
                out[lower, first] = -imag_part


def product_kernel(row_parts, group, chips, *refs):
    count = row_parts * chips
    sides, high, low, outs = refs[:count], refs[count], refs[count + 1], refs[count + 2 :]
    left = jnp.concatenate(
        [
            jnp.concatenate([sides[gap * row_parts + part][at] for at in (0, 1) for part in range(row_parts)], axis=1)
            for gap in range(chips)
        ],
        axis=0,
    )
    left_high, left_low = split(left)
    cols = outs[0].shape[-1]
    for at in range(2):
        for gap in range(group):
            spot = pl.ds((at * group + gap) * cols, cols)
            right_high, right_low = high[:, spot], low[:, spot]
            dot = functools.partial(jnp.dot, preferred_element_type=jnp.float32)
            outs[gap][at] = dot(left_high, right_high) + (dot(left_high, right_low) + dot(left_low, right_high))


def final_kernel(group, chips, sizes, *refs):
    count = len(sizes) * group
    parts, less, collision, after = refs[:count], refs[count], refs[-2], refs[-1]
    chip = lax.axis_index("ka") // CORES
    base = 0
    for at, step in enumerate(sizes):
        for gap in range(chips):
            start = base + lax.rem(chip - gap + chips, chips) * step
            rows = pl.ds(pl.multiple_of(start, SUBLANES), step)
            spot = pl.ds(gap * step, step)
            total = parts[at * group][:, spot, :]
            for part in parts[at * group + 1 : (at + 1) * group]:
                total = total + part[:, spot, :]
            collision[:, 0, rows, :] = total
            after[:, 0, rows, :] = less[:, 0, rows, :] + total
        base += chips * step


def call(kernel, out_shapes, in_specs, out_specs, args, scratch=(), after=(), limit=VMEM_LIMIT, aliases=None):
    count, skipped = len(args), len(after)

    def ordered(*refs):
        kernel(*refs[:count], *refs[count + skipped :])

    return pl.pallas_call(
        ordered,
        out_shape=out_shapes,
        in_specs=in_specs + [ANYWHERE] * skipped,
        out_specs=out_specs,
        scratch_shapes=scratch,
        input_output_aliases=aliases or {},
        cost_estimate=pl.CostEstimate(flops=1, bytes_accessed=1, transcendentals=0),
        compiler_params=pltpu.CompilerParams(vmem_limit_bytes=limit),
    )(*args, *after)


def body(green_less, green_great, screened):
    momenta, row_parts, col_parts = lax.axis_size("ka"), lax.axis_size("tr"), lax.axis_size("tc")
    member = lax.axis_index("tc") % (col_parts // row_parts)
    rows, cols = green_less.shape[2], green_less.shape[3]
    group, chips = col_parts // row_parts, momenta // CORES
    sizes = chunk_sizes(rows // chips // SUBLANES)
    bases = [chips * sum(sizes[:at]) for at in range(len(sizes))]
    f32 = functools.partial(jax.ShapeDtypeStruct, dtype=jnp.float32)
    bf16 = functools.partial(jax.ShapeDtypeStruct, dtype=jnp.bfloat16)
    inputs = (green_less, green_great, screened)
    scale = momenta**-1.5 * (rows * row_parts) ** -0.5
    tables = jnp.asarray(angle_tables(momenta))

    def to_chip(value, gap):
        moves = [
            (chip * CORES + core, (chip + gap) % chips * CORES + core) for chip in range(chips) for core in range(CORES)
        ]
        return lax.ppermute(value, "ka", moves)

    def to_core(value):
        return lax.ppermute(value, "ka", [(s, s + 1 - 2 * (s % CORES)) for s in range(momenta)])

    def to_panel(value, rows_on, cols_on):
        moves = []
        for i in range(row_parts):
            for j in range(col_parts):
                column = j // group * group + (j + cols_on) % group
                moves.append((i * col_parts + j, (i + rows_on) % row_parts * col_parts + column))
        return lax.ppermute(value, ("tr", "tc"), moves)

    def to_half(value, gap):
        return lax.ppermute(value, "tc", [(j, (j + group * gap) % col_parts) for j in range(col_parts)])

    def pack(at, passed, after):
        step, count = sizes[at], len(passed)
        outs = call(
            functools.partial(pack_kernel, chips, bases[at], step, count),
            [f32(value.shape) for value in passed] + [f32((3, 2, step, cols))] * chips,
            [IN_HBM] * 3 + [ANYWHERE] * count,
            [ANYWHERE] * count + [ANYWHERE if at else IN_VMEM] * chips,
            (*inputs, *passed),
            [pltpu.SemaphoreType.DMA((3 * chips,))],
            after,
            FIRST_LIMIT if at == 0 else VMEM_LIMIT,
            {3 + spot: spot for spot in range(count)},
        )
        return outs[count:], outs[:count]

    def gate(passed, after):
        count = len(passed)
        return call(
            lambda *refs: None,
            [f32(value.shape) for value in passed],
            [ANYWHERE] * count,
            [ANYWHERE] * count,
            passed,
            (),
            after,
            aliases={spot: spot for spot in range(count)},
        )

    def forward(pieces):
        return [to_chip(pieces[gap], -gap) for gap in range(1, chips)], to_core(pieces[0])

    def energy(at, here, other, after):
        return call(
            functools.partial(energy_kernel, chips, scale),
            [f32((2, sizes[at], cols))] * chips,
            [IN_SMEM] + [IN_VMEM] * momenta,
            [IN_VMEM] * chips,
            (tables, *here, *other),
            (),
            after,
        )

    def product(at, lefts, after):
        outs = call(
            functools.partial(product_kernel, row_parts, group, chips),
            [f32((2, chips * sizes[at], cols))] * group,
            [IN_VMEM] * (len(lefts) + 2),
            [IN_VMEM] * group,
            (*lefts, *right),
            (),
            after,
        )
        return [outs[0]] + [to_panel(outs[gap], 0, -gap) for gap in range(1, group)]

    pieces = [pack(0, (), ())[0]]
    sent = [forward(pieces[0])]

    blocks = green_less[:, 0].reshape(2, group, cols, cols)
    panels = []
    for rows_on in range(row_parts):
        for cols_on in range(group):
            block = lax.dynamic_index_in_dim(blocks, (member + cols_on) % group, 1, False)
            panels.append(to_panel(block, rows_on, cols_on) if rows_on + cols_on else block)
    extent = 2 * row_parts * cols

    lefts, results, last, arrived, returned = [], [], (), (), ()
    for at in range(len(sizes) + 1):
        if at < len(sizes):
            across, beside = sent[at]
            if at + 1 < len(sizes):
                fresh, across = pack(at + 1, across, (*arrived, *last))
                pieces.append(fresh)
                sent.append(forward(fresh))
            else:
                across = gate(across, (*arrived, *last, *(results[-2][1:] if len(results) > 1 else ())))
            gates = () if at else panels[1 : group + 1]
            if at == 1:
                right = call(
                    functools.partial(right_kernel, row_parts, group),
                    [bf16((extent, 2 * group * cols))] * 2,
                    [IN_VMEM] * len(panels),
                    [IN_VMEM] * 2,
                    panels,
                    (),
                    across,
                )
                gates = right
            here = [pieces[at][0], *across]
            other = [beside, *(to_core(piece) for piece in across)]
            sigmas = energy(at, here, other, gates)
            owned = [sigmas[0]] + [to_chip(sigmas[gap], gap) for gap in range(1, chips)]
            lefts.append([part for own in owned for part in [own] + [to_half(own, gap) for gap in range(1, row_parts)]])
            returned = owned[1:2]
            arrived = (*returned, *lefts[at][1:2])
            if at == 0:
                arrived += (*panels[group + 1 :], *lefts[at][row_parts + 1 : 2 * row_parts])
            last = sigmas[:1]
        if at >= 1:
            before = results[-2][1:] if len(results) > 1 else ()
            gates = (*last, *((*returned, *lefts[at][1:2]) if at + 1 == len(sizes) else ()), *before)
            results.append(product(at - 1, lefts[at - 1], gates))
            last, returned = results[-1][:1], ()

    return call(
        functools.partial(final_kernel, group, chips, sizes),
        [f32(green_less.shape)] * 2,
        [IN_VMEM] * (len(sizes) * group + 1),
        [IN_VMEM] * 2,
        (*[part for result in results for part in result], green_less),
    )


def solution(mesh):
    spec = P(None, "ka", "tr", "tc")
    return jax.shard_map(body, mesh=mesh, in_specs=(spec,) * 3, out_specs=(spec,) * 2, check_vma=False)
```
